32 devices in a mesh: row: 8 (over y, x, core), col: 4 (over z).
Axes of the slice: x: 2, y: 2, z: 4, core: 2. Of those that a mesh axis runs over, the one named last changes fastest.
Arguments:
- front_init: float32 [16, 16, 2, 1024], P(None, None, None, 'row'), may hold values from -3 to 3
- green_hist: float32 [64, 16, 2, 1024], P('row', None, None, 'col'), may hold values from -0.125 to 0.125
- field_hist: float32 [64, 16, 2, 1024], P('row', None, None, 'col'), may hold values from -0.125 to 0.125
Outputs:
- front_final: float32 [16, 16, 2, 1024], P(None, None, None, 'row')
The draws below stay inside these ranges and needn't reach their ends.
All inputs are finite; a program needn't handle non-finite values.
Results may differ from the reference program's by a relative error of at most 0.0001.
Values sent between devices are 32-bit elements; how exact they have to be, the bound alone decides.
A program may use at most 64 MiB of HBM per device.

```python
import jax
import jax.numpy as jnp
from jax import lax

NO = 16
FR = 16
ITERS = 2
NT = 64


def block_scale(rng, shape, cuts, least, top_value):
    def one(axis_at, shards_of):
        heights = jax.random.uniform(jax.random.fold_in(jax.random.fold_in(rng, 6), axis_at), (shards_of,), jnp.float32, least / len(cuts), top_value / len(cuts))
        return jnp.repeat(jnp.exp(heights), shape[axis_at] // shards_of).reshape((-1,) + (1,) * (len(shape) - axis_at - 1))

    level = one(*cuts[0])
    for cut in cuts[1:]:
        level = level * one(*cut)
    return level


def bell_draw(own_key, shape, width, most, cuts=(), held_as=jnp.bfloat16):
    drawn = width * jax.random.normal(own_key, shape, jnp.float32)
    if cuts:
        drawn = drawn * block_scale(own_key, shape, cuts, -0.22, 0.18)
    return jnp.clip(drawn, -most, most).astype(held_as)


def setup_inputs(seed: int = 0) -> dict:
    arg_keys = jax.random.split(jax.random.key(seed), 4)
    front_init = bell_draw(arg_keys[0], (FR, NO, 2, NT * NO), 0.5, 3.0, ((3, 8),), jnp.float32)
    green_hist = bell_draw(arg_keys[1], (NT, NO, 2, NT * NO), (2 * NT * NO) ** -0.5, 0.125, ((0, 8), (3, 4)), jnp.float32)
    field_hist = bell_draw(arg_keys[2], (NT, NO, 2, NT * NO), (2 * NT * NO) ** -0.5, 0.125, ((0, 8), (3, 4)), jnp.float32)
    return dict(front_init=front_init, green_hist=green_hist, field_hist=field_hist)


STEP_WEIGHT = 0.5


def product(left, right):
    return jnp.dot(left, right, precision=lax.Precision.HIGHEST, preferred_element_type=jnp.float32)


def cubic_sigma(current):
    count, orbits, parts, length = current.shape
    swapped = current.reshape(count, orbits, parts, length // orbits, orbits)
    swapped = swapped.transpose(0, 4, 2, 3, 1).reshape(current.shape)
    real_part = current[:, :, 0, :]
    imag_part = current[:, :, 1, :]
    square_re = real_part * real_part - imag_part * imag_part
    square_im = 2.0 * real_part * imag_part
    other_re = swapped[:, :, 0, :]
    other_im = swapped[:, :, 1, :]
    sigma_re = square_re * other_re + square_im * other_im
    sigma_im = square_im * other_re - square_re * other_im
    return sigma_re, sigma_im


def collide(current, green_re, green_im, field_re, field_im):
    count, orbits, parts, length = current.shape
    sigma_re, sigma_im = cubic_sigma(current)
    sigma_re = sigma_re.reshape(count * orbits, length)
    sigma_im = sigma_im.reshape(count * orbits, length)
    front_re = current[:, :, 0, :].reshape(count * orbits, length)
    front_im = current[:, :, 1, :].reshape(count * orbits, length)
    image_re = product(sigma_re, green_re) - product(sigma_im, green_im) + product(front_re, field_re) - product(front_im, field_im)
    image_im = product(sigma_re, green_im) + product(sigma_im, green_re) + product(front_re, field_im) + product(front_im, field_re)
    image_re = image_re.reshape(count, orbits, -1)
    image_im = image_im.reshape(count, orbits, -1)
    return jnp.stack([image_re, image_im], axis=2)


def matrices(history):
    rows = history.shape[0] * history.shape[1]
    return history[:, :, 0, :].reshape(rows, -1), history[:, :, 1, :].reshape(rows, -1)


def reference(front_init, green_hist, field_hist):
    green_re, green_im = matrices(green_hist)
    field_re, field_im = matrices(field_hist)
    current = front_init
    for sweep in range(ITERS):
        current = front_init + STEP_WEIGHT * collide(current, green_re, green_im, field_re, field_im)
    return current
```

```python
import functools

import jax
import jax.numpy as jnp
from jax import lax
from jax.experimental import pallas as pl
from jax.experimental.pallas import tpu as pltpu
from jax.sharding import PartitionSpec as P

ITERS = 2
STEP_WEIGHT = 0.5
MOST_CHUNKS = 4
MESH = pl.DeviceIdType.MESH


def split(value):
    high = value.astype(jnp.bfloat16)
    low = (value - high.astype(jnp.float32)).astype(jnp.bfloat16)
    return high, low


def swap_orbits(real_part, imag_part, orbits):
    rows, lanes = real_part.shape
    blocks = lanes // orbits
    turned = jnp.concatenate([real_part, imag_part], axis=0).T
    pieces = [turned[at * orbits:(at + 1) * orbits] for at in range(blocks)]
    block_of_lane = lax.broadcasted_iota(jnp.int32, (orbits, lanes), 1) // orbits
    step = 1
    while step < blocks:
        low_side = (block_of_lane // step) % 2 == 0
        for at in range(blocks):
            if at & step:
                continue
            first, second = pieces[at], pieces[at + step]
            pieces[at] = jnp.where(low_side, first, pltpu.roll(second, step * orbits, 1))
            pieces[at + step] = jnp.where(low_side, pltpu.roll(first, lanes - step * orbits, 1), second)
        step *= 2
    whole = jnp.concatenate(pieces, axis=0)
    return whole[:rows], whole[rows:]


def cubic_sigma(real_part, imag_part, orbits):
    other_re, other_im = swap_orbits(real_part, imag_part, orbits)
    square_re = real_part * real_part - imag_part * imag_part
    square_im = 2.0 * real_part * imag_part
    return square_re * other_re + square_im * other_im, square_im * other_re - square_re * other_im


def kernel(
    n, chunks, orbits,
    front_ref, green_ref, field_ref, out_ref,
    b_high, b_low, pair_out, pair_in, own, rs_out, rs_in, total, z_in, done,
    pair_ss, pair_rs, rs_ss, rs_rs, z_ss, z_rs, done_ss, done_rs,
):
    row, plane = lax.axis_index("row"), lax.axis_index("col")
    chip, core = row // 2, row % 2
    rows, lanes = front_ref.shape[0] // 2, front_ref.shape[1]
    chunk_rows = rows // chunks
    unit = chunk_rows // n
    group = lanes // 2

    def at_chip(other):
        return (other * 2 + core, plane)

    def at_plane(other):
        return (row, other)

    sibling = (chip * 2 + 1 - core, plane)
    chips = [lax.rem(chip + d, n) for d in range(n)]
    planes = [lax.rem(plane + d, n) for d in range(n)]

    barrier = pltpu.get_barrier_semaphore()
    peers = [sibling] + [at_chip(chips[d]) for d in range(1, n)] + [at_plane(planes[d]) for d in range(1, n)]
    for peer in peers:
        pl.semaphore_signal(barrier, inc=1, device_id=peer, device_id_type=MESH)

    depth = green_ref.shape[0] // 4
    for half in range(2):
        at = 0
        for history in (green_ref, field_ref):
            real_part = history[pl.ds(2 * half, depth, stride=4), :]
            imag_part = history[pl.ds(2 * half + 1, depth, stride=4), :]
            real_high, real_low = split(real_part)
            imag_high, imag_low = split(imag_part)
            for store, re, im in ((b_high, real_high, imag_high), (b_low, real_low, imag_low)):
                store[half, at:at + depth, :lanes] = re
                store[half, at:at + depth, lanes:] = im
                store[half, at + depth:at + 2 * depth, :lanes] = -im
                store[half, at + depth:at + 2 * depth, lanes:] = re
            at += 2 * depth

    def remote(src, dst, send_sem, recv_sem, device):
        return pltpu.make_async_remote_copy(
            src_ref=src, dst_ref=dst, send_sem=send_sem, recv_sem=recv_sem, device_id=device, device_id_type=MESH
        )

    def pair_copy(it, h):
        return remote(pair_out.at[it, h], pair_in.at[it, h], pair_ss.at[it, h], pair_rs.at[it, h], sibling)

    def rs_copy(it, h, d):
        to = chips[d]
        return remote(rs_out.at[it, h, to], rs_in.at[it, h, d], rs_ss.at[it, h, d], rs_rs.at[it, h, d], at_chip(to))

    def z_copy(it, h, d):
        return remote(total.at[it, h], z_in.at[it, h, plane], z_ss.at[it, h, d], z_rs.at[it, h, plane], at_plane(planes[d]))

    def z_done_copy(it, h, d):
        return remote(total.at[it, h], done.at[it, h, chip], z_ss.at[it, h, d], done_rs.at[it, h, chip], at_plane(planes[d]))

    def done_copy(it, h, to, src):
        return remote(src, done.at[it, h, chip], done_ss.at[it, h, to], done_rs.at[it, h, chip], at_chip(to))

    def front(h, part):
        return front_ref[pl.ds(2 * h * chunk_rows + part, chunk_rows, stride=2), :]

    def arrived(it, h, part):
        return jnp.concatenate([done[it, h, p, part] for p in range(n)], axis=0)

    def current(it, h):
        if it == 0:
            return front(h, 0), front(h, 1)
        return tuple(front(h, part) + STEP_WEIGHT * arrived(it - 1, h, part) for part in range(2))

    def multiply(it, h):
        real_part, imag_part = current(it, h)
        sigmas = [
            cubic_sigma(real_part[at:at + group], imag_part[at:at + group], orbits)
            for at in range(0, chunk_rows, group)
        ]
        sigma_re = jnp.concatenate([s[0] for s in sigmas], axis=0)
        sigma_im = jnp.concatenate([s[1] for s in sigmas], axis=0)
        high, low = split(jnp.concatenate([sigma_re, sigma_im, real_part, imag_part], axis=1))
        both = jnp.concatenate([high, low], axis=0)
        for half, store in ((1 - core, pair_out.at[it]), (core, own)):
            upper = jnp.dot(both, b_high[half], preferred_element_type=jnp.float32)
            image = upper[:chunk_rows] + upper[chunk_rows:]
            image = image + jnp.dot(high, b_low[half], preferred_element_type=jnp.float32)
            store[h, 0] = image[:, :lanes]
            store[h, 1] = image[:, lanes:]
            if store is not own:
                if it == 0 and h == 0:
                    pl.semaphore_wait(barrier, len(peers))
                pair_copy(it, h).start()

    def add_pair(it, h):
        pair_copy(it, h).wait_recv()
        for d in list(range(1, n)) + [0]:
            to = chips[d]
            place = pl.ds(pl.multiple_of(to * unit, unit), unit)
            for part in range(2):
                rs_out[it, h, to, part] = own[h, part, place, :] + pair_in[it, h, part, place, :]
            if d:
                rs_copy(it, h, d).start()

    def add_chips(it, h):
        for d in range(1, n):
            rs_copy(it, h, d).wait_recv()
        value = rs_out[it, h, chip]
        for d in range(1, n):
            value = value + rs_in[it, h, d]
        total[it, h] = value

        @pl.when(chip == plane)
        def _():
            for d in range(1, n):
                z_done_copy(it, h, d).start()
            done[it, h, chip] = value

        @pl.when(chip != plane)
        def _():
            for d in range(1, n):
                z_copy(it, h, d).start()
            done_copy(it, h, plane, total.at[it, h]).start()

    def forward(it, h):
        for d in range(1, n):
            to = chips[d]

            @pl.when(to != plane)
            def _():
                landed = z_in.at[it, h, to]
                remote(landed, landed, z_ss.at[it, h, d], z_rs.at[it, h, to], at_plane(to)).wait_recv()
                done_copy(it, h, to, landed).start()

    def settle(it, h):
        for d in range(1, n):
            source = chips[d]
            landed = done.at[it, h, source]
            remote(landed, landed, done_ss.at[it, h, source], done_rs.at[it, h, source], at_chip(source)).wait_recv()

        @pl.when(chip != plane)
        def _():
            landed = done.at[it, h, chip]
            remote(landed, landed, done_ss.at[it, h, chip], done_rs.at[it, h, chip], at_plane(chip)).wait_recv()

    def finish(it, h):
        settle(it, h)
        if it == ITERS - 1:
            for part in range(2):
                place = pl.ds(2 * h * chunk_rows + part, chunk_rows, stride=2)
                out_ref[place, :] = front(h, part) + STEP_WEIGHT * arrived(it, h, part)

    stages = (multiply, add_pair, add_chips, forward, finish)
    tasks = [
        (it * len(stages) + at + h, it, at, h)
        for it in range(ITERS) for at in range(len(stages)) for h in range(chunks)
    ]
    for _, it, at, h in sorted(tasks, key=lambda task: (task[0], task[3])):
        stages[at](it, h)

    for it in range(ITERS):
        for h in range(chunks):
            pair_copy(it, h).wait_send()
            for d in range(1, n):
                rs_copy(it, h, d).wait_send()
                z_copy(it, h, d).wait_send()
                done_copy(it, h, chips[d], total.at[it, h]).wait_send()


def per_device(front_init, green_hist, field_hist):
    n = lax.axis_size("col")
    if lax.axis_size("row") != 2 * n or green_hist.shape[3] != 2 * front_init.shape[3]:
        raise ValueError("unexpected mesh")
    count, orbits, parts, lanes = front_init.shape
    rows = count * orbits
    chunks = max(1, min(MOST_CHUNKS, rows // (8 * n), 2 * rows // lanes))
    unit = rows // (chunks * n)

    def flat(history):
        steps, depth = history.shape[:2]
        return history.reshape(steps * depth, parts, 2, lanes).transpose(0, 2, 1, 3).reshape(-1, lanes)

    def vmem(*shape):
        return pltpu.VMEM(shape, jnp.float32)

    depth = green_hist.shape[0] * green_hist.shape[1]
    lead = (ITERS, chunks)
    sems = lambda *shape: pltpu.SemaphoreType.DMA(shape)
    result = pl.pallas_call(
        functools.partial(kernel, n, chunks, orbits),
        out_shape=jax.ShapeDtypeStruct((rows * parts, lanes), jnp.float32),
        in_specs=[pl.BlockSpec(memory_space=pltpu.VMEM)] * 3,
        out_specs=pl.BlockSpec(memory_space=pltpu.VMEM),
        scratch_shapes=[
            pltpu.VMEM((2, 4 * depth, 2 * lanes), jnp.bfloat16),
            pltpu.VMEM((2, 4 * depth, 2 * lanes), jnp.bfloat16),
            vmem(*lead, 2, rows // chunks, lanes),
            vmem(*lead, 2, rows // chunks, lanes),
            vmem(chunks, 2, rows // chunks, lanes),
            vmem(*lead, n, 2, unit, lanes),
            vmem(*lead, n, 2, unit, lanes),
            vmem(*lead, 2, unit, lanes),
            vmem(*lead, n, 2, unit, lanes),
            vmem(*lead, n, 2, unit, lanes),
            sems(*lead), sems(*lead),
            sems(*lead, n), sems(*lead, n),
            sems(*lead, n), sems(*lead, n),
            sems(*lead, n), sems(*lead, n),
        ],
        compiler_params=pltpu.CompilerParams(
            collective_id=0, has_side_effects=True, vmem_limit_bytes=40 * 1024 * 1024
        ),
    )(front_init.reshape(rows * parts, lanes), flat(green_hist), flat(field_hist))
    return result.reshape(front_init.shape)


def solution(mesh):
    in_specs = (
        P(None, None, None, "row"),
        P("row", None, None, "col"),
        P("row", None, None, "col"),
    )
    out_specs = P(None, None, None, "row")
    return jax.shard_map(
        per_device, mesh=mesh, in_specs=in_specs, out_specs=out_specs, check_vma=False
    )
```

```python
import functools

import jax
import jax.numpy as jnp
from jax import lax
from jax.experimental import pallas as pl
from jax.experimental.pallas import tpu as pltpu
from jax.sharding import PartitionSpec as P

ITERS = 2
STEP_WEIGHT = 0.5
MOST_CHUNKS = 2
MESH = pl.DeviceIdType.MESH


def split(value):
    high = value.astype(jnp.bfloat16)
    low = (value - high.astype(jnp.float32)).astype(jnp.bfloat16)
    return high, low


def swap_orbits(real_part, imag_part, orbits):
    rows, lanes = real_part.shape
    blocks = lanes // orbits
    turned = jnp.concatenate([real_part, imag_part], axis=0).T
    pieces = [turned[at * orbits:(at + 1) * orbits] for at in range(blocks)]
    block_of_lane = lax.broadcasted_iota(jnp.int32, (orbits, lanes), 1) // orbits
    step = 1
    while step < blocks:
        low_side = (block_of_lane // step) % 2 == 0
        for at in range(blocks):
            if at & step:
                continue
            first, second = pieces[at], pieces[at + step]
            pieces[at] = jnp.where(low_side, first, pltpu.roll(second, step * orbits, 1))
            pieces[at + step] = jnp.where(low_side, pltpu.roll(first, lanes - step * orbits, 1), second)
        step *= 2
    whole = jnp.concatenate(pieces, axis=0)
    return whole[:rows], whole[rows:]


def cubic_sigma(real_part, imag_part, orbits):
    other_re, other_im = swap_orbits(real_part, imag_part, orbits)
    square_re = real_part * real_part - imag_part * imag_part
    square_im = 2.0 * real_part * imag_part
    return square_re * other_re + square_im * other_im, square_im * other_re - square_re * other_im


def kernel(
    n, chunks, orbits,
    front_hbm, green_hbm, field_hbm, out_ref,
    front_ref, green_ref, field_ref, load_sem, b_high, b_low, pair_out, pair_in, own, rs_out, rs_in, total, z_in, done,
    pair_ss, pair_rs, rs_ss, rs_rs, z_ss, z_rs, done_ss, done_rs,
):
    row, plane = lax.axis_index("row"), lax.axis_index("col")
    chip, core = row // 2, row % 2
    rows, lanes = front_ref.shape[0] // 2, front_ref.shape[1]
    chunk_rows = rows // chunks
    unit = chunk_rows // n
    group = lanes // 2

    def at_chip(other):
        return (other * 2 + core, plane)

    def at_plane(other):
        return (row, other)

    sibling = (chip * 2 + 1 - core, plane)
    chips = [lax.rem(chip + d, n) for d in range(n)]
    planes = [lax.rem(plane + d, n) for d in range(n)]

    loads = [
        pltpu.make_async_copy(src, dst, load_sem.at[at])
        for at, (src, dst) in enumerate(((green_hbm, green_ref), (field_hbm, field_ref), (front_hbm, front_ref)))
    ]
    for load in loads:
        load.start()

    barrier = pltpu.get_barrier_semaphore()
    peers = [sibling] + [at_chip(chips[d]) for d in range(1, n)] + [at_plane(planes[d]) for d in range(1, n)]
    for peer in peers:
        pl.semaphore_signal(barrier, inc=1, device_id=peer, device_id_type=MESH)

    for load in loads:
        load.wait()
    depth = green_ref.shape[0] // 4
    for half in range(2):
        at = 0
        for history in (green_ref, field_ref):
            real_part = history[pl.ds(2 * half, depth, stride=4), :]
            imag_part = history[pl.ds(2 * half + 1, depth, stride=4), :]
            real_high, real_low = split(real_part)
            imag_high, imag_low = split(imag_part)
            for store, re, im in ((b_high, real_high, imag_high), (b_low, real_low, imag_low)):
                store[half, at:at + depth, :lanes] = re
                store[half, at:at + depth, lanes:] = im
                store[half, at + depth:at + 2 * depth, :lanes] = -im
                store[half, at + depth:at + 2 * depth, lanes:] = re
            at += 2 * depth

    def remote(src, dst, send_sem, recv_sem, device):
        return pltpu.make_async_remote_copy(
            src_ref=src, dst_ref=dst, send_sem=send_sem, recv_sem=recv_sem, device_id=device, device_id_type=MESH
        )

    def pair_copy(it, h):
        return remote(pair_out.at[it, h], pair_in.at[it, h], pair_ss.at[it, h], pair_rs.at[it, h], sibling)

    def rs_copy(it, h, d):
        to = chips[d]
        return remote(rs_out.at[it, h, to], rs_in.at[it, h, d], rs_ss.at[it, h, d], rs_rs.at[it, h, d], at_chip(to))

    def z_copy(it, h, d):
        return remote(total.at[it, h], z_in.at[it, h, plane], z_ss.at[it, h, d], z_rs.at[it, h, plane], at_plane(planes[d]))

    def z_done_copy(it, h, d):
        return remote(total.at[it, h], done.at[it, h, chip], z_ss.at[it, h, d], done_rs.at[it, h, chip], at_plane(planes[d]))

    def done_copy(it, h, to, src):
        return remote(src, done.at[it, h, chip], done_ss.at[it, h, to], done_rs.at[it, h, chip], at_chip(to))

    def front(h, part):
        return front_ref[pl.ds(2 * h * chunk_rows + part, chunk_rows, stride=2), :]

    def arrived(it, h, part):
        return jnp.concatenate([done[it, h, p, part] for p in range(n)], axis=0)

    def current(it, h):
        if it == 0:
            return front(h, 0), front(h, 1)
        return tuple(front(h, part) + STEP_WEIGHT * arrived(it - 1, h, part) for part in range(2))

    def multiply(it, h):
        real_part, imag_part = current(it, h)
        sigmas = [
            cubic_sigma(real_part[at:at + group], imag_part[at:at + group], orbits)
            for at in range(0, chunk_rows, group)
        ]
        sigma_re = jnp.concatenate([s[0] for s in sigmas], axis=0)
        sigma_im = jnp.concatenate([s[1] for s in sigmas], axis=0)
        high, low = split(jnp.concatenate([sigma_re, sigma_im, real_part, imag_part], axis=1))
        both = jnp.concatenate([high, low], axis=0)
        for half, store in ((1 - core, pair_out.at[it]), (core, own)):
            upper = jnp.dot(both, b_high[half], preferred_element_type=jnp.float32)
            image = upper[:chunk_rows] + upper[chunk_rows:]
            image = image + jnp.dot(high, b_low[half], preferred_element_type=jnp.float32)
            store[h, 0] = image[:, :lanes]
            store[h, 1] = image[:, lanes:]
            if store is not own:
                if it == 0 and h == 0:
                    pl.semaphore_wait(barrier, len(peers))
                pair_copy(it, h).start()

    def add_pair(it, h):
        pair_copy(it, h).wait_recv()
        for d in list(range(1, n)) + [0]:
            to = chips[d]
            place = pl.ds(pl.multiple_of(to * unit, unit), unit)
            for part in range(2):
                rs_out[it, h, to, part] = own[h, part, place, :] + pair_in[it, h, part, place, :]
            if d:
                rs_copy(it, h, d).start()

    def add_chips(it, h):
        for d in range(1, n):
            rs_copy(it, h, d).wait_recv()
        value = rs_out[it, h, chip]
        for d in range(1, n):
            value = value + rs_in[it, h, d]
        total[it, h] = value

        @pl.when(chip == plane)
        def _():
            for d in range(1, n):
                z_done_copy(it, h, d).start()
            done[it, h, chip] = value

        @pl.when(chip != plane)
        def _():
            for d in range(1, n):
                z_copy(it, h, d).start()
            done_copy(it, h, plane, total.at[it, h]).start()

    def forward(it, h):
        for d in range(1, n):
            to = chips[d]

            @pl.when(to != plane)
            def _():
                landed = z_in.at[it, h, to]
                remote(landed, landed, z_ss.at[it, h, d], z_rs.at[it, h, to], at_plane(to)).wait_recv()
                done_copy(it, h, to, landed).start()

    def settle(it, h):
        for d in range(1, n):
            source = chips[d]
            landed = done.at[it, h, source]
            remote(landed, landed, done_ss.at[it, h, source], done_rs.at[it, h, source], at_chip(source)).wait_recv()

        @pl.when(chip != plane)
        def _():
            landed = done.at[it, h, chip]
            remote(landed, landed, done_ss.at[it, h, chip], done_rs.at[it, h, chip], at_plane(chip)).wait_recv()

    def finish(it, h):
        settle(it, h)
        if it == ITERS - 1:
            for part in range(2):
                place = pl.ds(2 * h * chunk_rows + part, chunk_rows, stride=2)
                out_ref[place, :] = front(h, part) + STEP_WEIGHT * arrived(it, h, part)

    stages = (multiply, add_pair, add_chips, forward, finish)
    tasks = [
        (it * len(stages) + at + h, it, at, h)
        for it in range(ITERS) for at in range(len(stages)) for h in range(chunks)
    ]
    for _, it, at, h in sorted(tasks, key=lambda task: (task[0], task[3])):
        stages[at](it, h)

    for it in range(ITERS):
        for h in range(chunks):
            pair_copy(it, h).wait_send()
            for d in range(1, n):
                rs_copy(it, h, d).wait_send()
                z_copy(it, h, d).wait_send()
                done_copy(it, h, chips[d], total.at[it, h]).wait_send()


def per_device(front_init, green_hist, field_hist):
    n = lax.axis_size("col")
    if lax.axis_size("row") != 2 * n or green_hist.shape[3] != 2 * front_init.shape[3]:
        raise ValueError("unexpected mesh")
    count, orbits, parts, lanes = front_init.shape
    rows = count * orbits
    chunks = max(1, min(MOST_CHUNKS, rows // (8 * n), 2 * rows // lanes))
    unit = rows // (chunks * n)

    def flat(history):
        steps, depth = history.shape[:2]
        return history.reshape(steps * depth, parts, 2, lanes).transpose(0, 2, 1, 3).reshape(-1, lanes)

    def vmem(*shape):
        return pltpu.VMEM(shape, jnp.float32)

    depth = green_hist.shape[0] * green_hist.shape[1]
    lead = (ITERS, chunks)
    sems = lambda *shape: pltpu.SemaphoreType.DMA(shape)
    result = pl.pallas_call(
        functools.partial(kernel, n, chunks, orbits),
        out_shape=jax.ShapeDtypeStruct((rows * parts, lanes), jnp.float32),
        in_specs=[pl.BlockSpec(memory_space=pl.ANY)] * 3,
        out_specs=pl.BlockSpec(memory_space=pltpu.VMEM),
        scratch_shapes=[
            vmem(rows * parts, lanes),
            vmem(4 * depth, lanes),
            vmem(4 * depth, lanes),
            sems(3),
            pltpu.VMEM((2, 4 * depth, 2 * lanes), jnp.bfloat16),
            pltpu.VMEM((2, 4 * depth, 2 * lanes), jnp.bfloat16),
            vmem(*lead, 2, rows // chunks, lanes),
            vmem(*lead, 2, rows // chunks, lanes),
            vmem(chunks, 2, rows // chunks, lanes),
            vmem(*lead, n, 2, unit, lanes),
            vmem(*lead, n, 2, unit, lanes),
            vmem(*lead, 2, unit, lanes),
            vmem(*lead, n, 2, unit, lanes),
            vmem(*lead, n, 2, unit, lanes),
            sems(*lead), sems(*lead),
            sems(*lead, n), sems(*lead, n),
            sems(*lead, n), sems(*lead, n),
            sems(*lead, n), sems(*lead, n),
        ],
        compiler_params=pltpu.CompilerParams(
            collective_id=0, has_side_effects=True, vmem_limit_bytes=56 * 1024 * 1024
        ),
    )(front_init.reshape(rows * parts, lanes), flat(green_hist), flat(field_hist))
    return result.reshape(front_init.shape)


def solution(mesh):
    in_specs = (
        P(None, None, None, "row"),
        P("row", None, None, "col"),
        P("row", None, None, "col"),
    )
    out_specs = P(None, None, None, "row")
    return jax.shard_map(
        per_device, mesh=mesh, in_specs=in_specs, out_specs=out_specs, check_vma=False
    )
```

```python
import functools

import jax
import jax.numpy as jnp
from jax import lax
from jax.experimental import pallas as pl
from jax.experimental.pallas import tpu as pltpu
from jax.sharding import PartitionSpec as P

ITERS = 2
STEP_WEIGHT = 0.5
MOST_CHUNKS = 2
MESH = pl.DeviceIdType.MESH


def split(value):
    high = value.astype(jnp.bfloat16)
    low = (value - high.astype(jnp.float32)).astype(jnp.bfloat16)
    return high, low


def swap_orbits(real_part, imag_part, orbits):
    rows, lanes = real_part.shape
    blocks = lanes // orbits
    turned = jnp.concatenate([real_part, imag_part], axis=0).T
    pieces = [turned[at * orbits:(at + 1) * orbits] for at in range(blocks)]
    block_of_lane = lax.broadcasted_iota(jnp.int32, (orbits, lanes), 1) // orbits
    step = 1
    while step < blocks:
        low_side = (block_of_lane // step) % 2 == 0
        for at in range(blocks):
            if at & step:
                continue
            first, second = pieces[at], pieces[at + step]
            pieces[at] = jnp.where(low_side, first, pltpu.roll(second, step * orbits, 1))
            pieces[at + step] = jnp.where(low_side, pltpu.roll(first, lanes - step * orbits, 1), second)
        step *= 2
    whole = jnp.concatenate(pieces, axis=0)
    return whole[:rows], whole[rows:]


def cubic_sigma(real_part, imag_part, orbits):
    other_re, other_im = swap_orbits(real_part, imag_part, orbits)
    square_re = real_part * real_part - imag_part * imag_part
    square_im = 2.0 * real_part * imag_part
    return square_re * other_re + square_im * other_im, square_im * other_re - square_re * other_im


def kernel(
    n, chunks, orbits,
    front_hbm, green_hbm, field_hbm, out_ref,
    front_ref, green_ref, field_ref, load_sem, b_high, b_low, pair_out, pair_in, own, rs_out, rs_in, total, done,
    pair_ss, pair_rs, rs_ss, rs_rs, done_ss, done_rs,
):
    row, plane = lax.axis_index("row"), lax.axis_index("col")
    chip, core = row // 2, row % 2
    rows, lanes = front_ref.shape[0] // 2, front_ref.shape[1]
    chunk_rows = rows // chunks
    unit = chunk_rows // n
    group = lanes // 2

    def at_chip(other):
        return (other * 2 + core, plane)

    sibling = (chip * 2 + 1 - core, plane)
    chips = [lax.rem(chip + d, n) for d in range(n)]
    planes = [lax.rem(plane + d, n) for d in range(n)]

    loads = [
        pltpu.make_async_copy(src, dst, load_sem.at[at])
        for at, (src, dst) in enumerate(((green_hbm, green_ref), (field_hbm, field_ref), (front_hbm, front_ref)))
    ]
    for load in loads:
        load.start()

    barrier = pltpu.get_barrier_semaphore()
    for source in [sibling] + [at_chip(chips[d]) for d in range(1, n)]:
        pl.semaphore_signal(barrier, inc=1, device_id=source, device_id_type=MESH)

    @pl.when(chip != plane)
    def _():
        for d in range(n):
            pl.semaphore_signal(barrier, inc=1, device_id=(chips[d] * 2 + core, chip), device_id_type=MESH)

    for load in loads:
        load.wait()
    depth = green_ref.shape[0] // 4
    for half in range(2):
        at = 0
        for history in (green_ref, field_ref):
            real_part = history[pl.ds(2 * half, depth, stride=4), :]
            imag_part = history[pl.ds(2 * half + 1, depth, stride=4), :]
            real_high, real_low = split(real_part)
            imag_high, imag_low = split(imag_part)
            for store, re, im in ((b_high, real_high, imag_high), (b_low, real_low, imag_low)):
                store[half, at:at + depth, :lanes] = re
                store[half, at:at + depth, lanes:] = im
                store[half, at + depth:at + 2 * depth, :lanes] = -im
                store[half, at + depth:at + 2 * depth, lanes:] = re
            at += 2 * depth

    def remote(src, dst, send_sem, recv_sem, device):
        return pltpu.make_async_remote_copy(
            src_ref=src, dst_ref=dst, send_sem=send_sem, recv_sem=recv_sem, device_id=device, device_id_type=MESH
        )

    def pair_copy(it, h):
        return remote(pair_out.at[it, h], pair_in.at[it, h], pair_ss.at[it, h], pair_rs.at[it, h], sibling)

    def rs_copy(it, h, d):
        to = chips[d]
        return remote(rs_out.at[it, h, to], rs_in.at[it, h, d], rs_ss.at[it, h, d], rs_rs.at[it, h, d], at_chip(to))

    def done_copy(it, h, d):
        to = (plane * 2 + core, planes[d])
        return remote(total.at[it, h], done.at[it, h, chip], done_ss.at[it, h, d], done_rs.at[it, h, chip], to)

    def front(h, part):
        return front_ref[pl.ds(2 * h * chunk_rows + part, chunk_rows, stride=2), :]

    def arrived(it, h, part):
        return jnp.concatenate([done[it, h, p, part] for p in range(n)], axis=0)

    def current(it, h):
        if it == 0:
            return front(h, 0), front(h, 1)
        return tuple(front(h, part) + STEP_WEIGHT * arrived(it - 1, h, part) for part in range(2))

    def multiply(it, h):
        real_part, imag_part = current(it, h)
        sigmas = [
            cubic_sigma(real_part[at:at + group], imag_part[at:at + group], orbits)
            for at in range(0, chunk_rows, group)
        ]
        sigma_re = jnp.concatenate([s[0] for s in sigmas], axis=0)
        sigma_im = jnp.concatenate([s[1] for s in sigmas], axis=0)
        high, low = split(jnp.concatenate([sigma_re, sigma_im, real_part, imag_part], axis=1))
        both = jnp.concatenate([high, low], axis=0)
        for half, store in ((1 - core, pair_out.at[it]), (core, own)):
            upper = jnp.dot(both, b_high[half], preferred_element_type=jnp.float32)
            image = upper[:chunk_rows] + upper[chunk_rows:]
            image = image + jnp.dot(high, b_low[half], preferred_element_type=jnp.float32)
            store[h, 0] = image[:, :lanes]
            store[h, 1] = image[:, lanes:]
            if store is not own:
                if it == 0 and h == 0:
                    pl.semaphore_wait(barrier, 2 * n - 1)
                pair_copy(it, h).start()

    def add_pair(it, h):
        pair_copy(it, h).wait_recv()
        for d in list(range(1, n)) + [0]:
            to = chips[d]
            place = pl.ds(pl.multiple_of(to * unit, unit), unit)
            for part in range(2):
                rs_out[it, h, to, part] = own[h, part, place, :] + pair_in[it, h, part, place, :]
            if d:
                rs_copy(it, h, d).start()

    def add_chips(it, h):
        for d in range(1, n):
            rs_copy(it, h, d).wait_recv()
        value = rs_out[it, h, chip]
        for d in range(1, n):
            value = value + rs_in[it, h, d]
        total[it, h] = value

        for d in range(1, n):
            done_copy(it, h, d).start()

        @pl.when(chip != plane)
        def _():
            done_copy(it, h, 0).start()

        @pl.when(chip == plane)
        def _():
            done[it, h, chip] = value

    def settle(it, h):
        for d in range(1, n):
            source = chips[d]
            landed = done.at[it, h, source]
            remote(landed, landed, done_ss.at[it, h, source], done_rs.at[it, h, source], at_chip(source)).wait_recv()

        @pl.when(chip != plane)
        def _():
            landed = done.at[it, h, chip]
            remote(landed, landed, done_ss.at[it, h, chip], done_rs.at[it, h, chip], (row, chip)).wait_recv()

    def finish(it, h):
        settle(it, h)
        if it == ITERS - 1:
            for part in range(2):
                place = pl.ds(2 * h * chunk_rows + part, chunk_rows, stride=2)
                out_ref[place, :] = front(h, part) + STEP_WEIGHT * arrived(it, h, part)

    stages = (multiply, add_pair, add_chips, finish)
    tasks = [
        (it * len(stages) + at + h, it, at, h)
        for it in range(ITERS) for at in range(len(stages)) for h in range(chunks)
    ]
    for _, it, at, h in sorted(tasks, key=lambda task: (task[0], task[3])):
        stages[at](it, h)

    for it in range(ITERS):
        for h in range(chunks):
            pair_copy(it, h).wait_send()
            for d in range(1, n):
                rs_copy(it, h, d).wait_send()
                done_copy(it, h, d).wait_send()

            @pl.when(chip != plane)
            def _():
                done_copy(it, h, 0).wait_send()


def per_device(front_init, green_hist, field_hist):
    n = lax.axis_size("col")
    if lax.axis_size("row") != 2 * n or green_hist.shape[3] != 2 * front_init.shape[3]:
        raise ValueError("unexpected mesh")
    count, orbits, parts, lanes = front_init.shape
    rows = count * orbits
    chunks = max(1, min(MOST_CHUNKS, rows // (8 * n), 2 * rows // lanes))
    unit = rows // (chunks * n)

    def flat(history):
        steps, depth = history.shape[:2]
        return history.reshape(steps * depth, parts, 2, lanes).transpose(0, 2, 1, 3).reshape(-1, lanes)

    def vmem(*shape):
        return pltpu.VMEM(shape, jnp.float32)

    depth = green_hist.shape[0] * green_hist.shape[1]
    lead = (ITERS, chunks)
    sems = lambda *shape: pltpu.SemaphoreType.DMA(shape)
    result = pl.pallas_call(
        functools.partial(kernel, n, chunks, orbits),
        out_shape=jax.ShapeDtypeStruct((rows * parts, lanes), jnp.float32),
        in_specs=[pl.BlockSpec(memory_space=pl.ANY)] * 3,
        out_specs=pl.BlockSpec(memory_space=pltpu.VMEM),
        scratch_shapes=[
            vmem(rows * parts, lanes),
            vmem(4 * depth, lanes),
            vmem(4 * depth, lanes),
            sems(3),
            pltpu.VMEM((2, 4 * depth, 2 * lanes), jnp.bfloat16),
            pltpu.VMEM((2, 4 * depth, 2 * lanes), jnp.bfloat16),
            vmem(*lead, 2, rows // chunks, lanes),
            vmem(*lead, 2, rows // chunks, lanes),
            vmem(chunks, 2, rows // chunks, lanes),
            vmem(*lead, n, 2, unit, lanes),
            vmem(*lead, n, 2, unit, lanes),
            vmem(*lead, 2, unit, lanes),
            vmem(*lead, n, 2, unit, lanes),
            sems(*lead), sems(*lead),
            sems(*lead, n), sems(*lead, n),
            sems(*lead, n), sems(*lead, n),
        ],
        compiler_params=pltpu.CompilerParams(
            collective_id=0, has_side_effects=True, vmem_limit_bytes=56 * 1024 * 1024
        ),
    )(front_init.reshape(rows * parts, lanes), flat(green_hist), flat(field_hist))
    return result.reshape(front_init.shape)


def solution(mesh):
    in_specs = (
        P(None, None, None, "row"),
        P("row", None, None, "col"),
        P("row", None, None, "col"),
    )
    out_specs = P(None, None, None, "row")
    return jax.shard_map(
        per_device, mesh=mesh, in_specs=in_specs, out_specs=out_specs, check_vma=False
    )
```

```python
import functools

import jax
import jax.numpy as jnp
from jax import lax
from jax.experimental import pallas as pl
from jax.experimental.pallas import tpu as pltpu
from jax.sharding import PartitionSpec as P

ITERS = 2
STEP_WEIGHT = 0.5
MOST_CHUNKS = 2
MESH = pl.DeviceIdType.MESH


def split(value):
    high = value.astype(jnp.bfloat16)
    low = (value - high.astype(jnp.float32)).astype(jnp.bfloat16)
    return high, low


def swap_orbits(real_part, imag_part, orbits):
    rows, lanes = real_part.shape
    blocks = lanes // orbits
    turned = jnp.concatenate([real_part, imag_part], axis=0).T
    pieces = [turned[at * orbits:(at + 1) * orbits] for at in range(blocks)]
    block_of_lane = lax.broadcasted_iota(jnp.int32, (orbits, lanes), 1) // orbits
    step = 1
    while step < blocks:
        low_side = (block_of_lane // step) % 2 == 0
        for at in range(blocks):
            if at & step:
                continue
            first, second = pieces[at], pieces[at + step]
            pieces[at] = jnp.where(low_side, first, pltpu.roll(second, step * orbits, 1))
            pieces[at + step] = jnp.where(low_side, pltpu.roll(first, lanes - step * orbits, 1), second)
        step *= 2
    whole = jnp.concatenate(pieces, axis=0)
    return whole[:rows], whole[rows:]


def cubic_sigma(real_part, imag_part, orbits):
    other_re, other_im = swap_orbits(real_part, imag_part, orbits)
    square_re = real_part * real_part - imag_part * imag_part
    square_im = 2.0 * real_part * imag_part
    return square_re * other_re + square_im * other_im, square_im * other_re - square_re * other_im


def kernel(
    n, chunks, orbits,
    front_hbm, green_hbm, field_hbm, out_ref,
    front_ref, green_ref, field_ref, load_sem, b_high, b_low, pair_out, pair_in, own, rs_out, rs_in, total, done,
    pair_ss, pair_rs, rs_ss, rs_rs, done_ss, done_rs,
):
    row, plane = lax.axis_index("row"), lax.axis_index("col")
    chip, core = row // 2, row % 2
    rows, lanes = front_ref.shape[0] // 2, front_ref.shape[1]
    chunk_rows = rows // chunks
    unit = chunk_rows // n
    group = lanes // 2

    def at_chip(other):
        return (other * 2 + core, plane)

    sibling = (chip * 2 + 1 - core, plane)
    chips = [lax.rem(chip + d, n) for d in range(n)]
    planes = [lax.rem(plane + d, n) for d in range(n)]

    loads = [
        pltpu.make_async_copy(src, dst, load_sem.at[at])
        for at, (src, dst) in enumerate(((green_hbm, green_ref), (field_hbm, field_ref), (front_hbm, front_ref)))
    ]
    for load in loads:
        load.start()

    barrier = pltpu.get_barrier_semaphore()
    for source in [sibling] + [at_chip(chips[d]) for d in range(1, n)]:
        pl.semaphore_signal(barrier, inc=1, device_id=source, device_id_type=MESH)

    @pl.when(chip != plane)
    def _():
        for d in range(n):
            pl.semaphore_signal(barrier, inc=1, device_id=(chips[d] * 2 + core, chip), device_id_type=MESH)

    for load in loads:
        load.wait()
    depth = green_ref.shape[0] // 4
    for half in range(2):
        at = 0
        for history in (green_ref, field_ref):
            real_part = history[pl.ds(2 * half, depth, stride=4), :]
            imag_part = history[pl.ds(2 * half + 1, depth, stride=4), :]
            real_high, real_low = split(real_part)
            imag_high, imag_low = split(imag_part)
            for store, re, im in ((b_high, real_high, imag_high), (b_low, real_low, imag_low)):
                store[half, at:at + depth, :lanes] = re
                store[half, at:at + depth, lanes:] = im
                store[half, at + depth:at + 2 * depth, :lanes] = -im
                store[half, at + depth:at + 2 * depth, lanes:] = re
            at += 2 * depth

    def remote(src, dst, send_sem, recv_sem, device):
        return pltpu.make_async_remote_copy(
            src_ref=src, dst_ref=dst, send_sem=send_sem, recv_sem=recv_sem, device_id=device, device_id_type=MESH
        )

    def pair_copy(it, h):
        return remote(pair_out.at[it, h], pair_in.at[it, h], pair_ss.at[it, h], pair_rs.at[it, h], sibling)

    def rs_copy(it, h, d):
        to = chips[d]
        return remote(rs_out.at[it, h, to], rs_in.at[it, h, d], rs_ss.at[it, h, d], rs_rs.at[it, h, d], at_chip(to))

    def done_copy(it, h, d):
        to = (plane * 2 + core, planes[d])
        return remote(total.at[it, h], done.at[it, h, chip], done_ss.at[it, h, d], done_rs.at[it, h, chip], to)

    def front(h, part):
        return front_ref[pl.ds(2 * h * chunk_rows + part, chunk_rows, stride=2), :]

    def arrived(it, h, part):
        return jnp.concatenate([done[it, h, p, part] for p in range(n)], axis=0)

    def current(it, h):
        if it == 0:
            return front(h, 0), front(h, 1)
        return tuple(front(h, part) + STEP_WEIGHT * arrived(it - 1, h, part) for part in range(2))

    def multiply(it, h):
        real_part, imag_part = current(it, h)
        sigmas = [
            cubic_sigma(real_part[at:at + group], imag_part[at:at + group], orbits)
            for at in range(0, chunk_rows, group)
        ]
        sigma_re = jnp.concatenate([s[0] for s in sigmas], axis=0)
        sigma_im = jnp.concatenate([s[1] for s in sigmas], axis=0)
        high, low = split(jnp.concatenate([sigma_re, sigma_im, real_part, imag_part], axis=1))
        both = jnp.concatenate([high, low], axis=0)
        for half, store in ((1 - core, pair_out.at[it]), (core, own)):
            upper = jnp.dot(both, b_high[half], preferred_element_type=jnp.float32)
            image = upper[:chunk_rows] + upper[chunk_rows:]
            image = image + jnp.dot(high, b_low[half], preferred_element_type=jnp.float32)
            store[h, 0] = image[:, :lanes]
            store[h, 1] = image[:, lanes:]
            if store is not own:
                if it == 0 and h == 0:
                    pl.semaphore_wait(barrier, 2 * n - 1)
                pair_copy(it, h).start()

    def add_pair(it, h):
        pair_copy(it, h).wait_recv()
        for d in list(range(1, n)) + [0]:
            to = chips[d]
            place = pl.ds(pl.multiple_of(to * unit, unit), unit)
            for part in range(2):
                rs_out[it, h, to, part] = own[h, part, place, :] + pair_in[it, h, part, place, :]
            if d:
                rs_copy(it, h, d).start()

    def add_chips(it, h):
        for d in range(1, n):
            rs_copy(it, h, d).wait_recv()
        value = rs_out[it, h, chip]
        for d in range(1, n):
            value = value + rs_in[it, h, d]
        total[it, h] = value

        for d in range(1, n):
            done_copy(it, h, d).start()

        @pl.when(chip != plane)
        def _():
            done_copy(it, h, 0).start()

        @pl.when(chip == plane)
        def _():
            done[it, h, chip] = value

    def settle(it, h):
        for d in range(1, n):
            source = chips[d]
            landed = done.at[it, h, source]
            remote(landed, landed, done_ss.at[it, h, source], done_rs.at[it, h, source], at_chip(source)).wait_recv()

        @pl.when(chip != plane)
        def _():
            landed = done.at[it, h, chip]
            remote(landed, landed, done_ss.at[it, h, chip], done_rs.at[it, h, chip], (row, chip)).wait_recv()

    def finish(it, h):
        settle(it, h)
        if it < ITERS - 1:
            multiply(it + 1, h)
        if it == ITERS - 1:
            for part in range(2):
                place = pl.ds(2 * h * chunk_rows + part, chunk_rows, stride=2)
                out_ref[place, :] = front(h, part) + STEP_WEIGHT * arrived(it, h, part)

    stages = (multiply, add_pair, add_chips, finish)
    tasks = [
        (it, at, h)
        for it in range(ITERS) for at in range(len(stages)) for h in range(chunks)
        if it == 0 or at > 0
    ]
    for it, at, h in tasks:
        stages[at](it, h)

    for it in range(ITERS):
        for h in range(chunks):
            pair_copy(it, h).wait_send()
            for d in range(1, n):
                rs_copy(it, h, d).wait_send()
                done_copy(it, h, d).wait_send()

            @pl.when(chip != plane)
            def _():
                done_copy(it, h, 0).wait_send()


def per_device(front_init, green_hist, field_hist):
    n = lax.axis_size("col")
    if lax.axis_size("row") != 2 * n or green_hist.shape[3] != 2 * front_init.shape[3]:
        raise ValueError("unexpected mesh")
    count, orbits, parts, lanes = front_init.shape
    rows = count * orbits
    chunks = max(1, min(MOST_CHUNKS, rows // (8 * n), 2 * rows // lanes))
    unit = rows // (chunks * n)

    def flat(history):
        steps, depth = history.shape[:2]
        return history.reshape(steps * depth, parts, 2, lanes).transpose(0, 2, 1, 3).reshape(-1, lanes)

    def vmem(*shape):
        return pltpu.VMEM(shape, jnp.float32)

    depth = green_hist.shape[0] * green_hist.shape[1]
    lead = (ITERS, chunks)
    sems = lambda *shape: pltpu.SemaphoreType.DMA(shape)
    result = pl.pallas_call(
        functools.partial(kernel, n, chunks, orbits),
        out_shape=jax.ShapeDtypeStruct((rows * parts, lanes), jnp.float32),
        in_specs=[pl.BlockSpec(memory_space=pltpu.HBM)] * 3,
        out_specs=pl.BlockSpec(memory_space=pltpu.VMEM),
        scratch_shapes=[
            vmem(rows * parts, lanes),
            vmem(4 * depth, lanes),
            vmem(4 * depth, lanes),
            sems(3),
            pltpu.VMEM((2, 4 * depth, 2 * lanes), jnp.bfloat16),
            pltpu.VMEM((2, 4 * depth, 2 * lanes), jnp.bfloat16),
            vmem(*lead, 2, rows // chunks, lanes),
            vmem(*lead, 2, rows // chunks, lanes),
            vmem(chunks, 2, rows // chunks, lanes),
            vmem(*lead, n, 2, unit, lanes),
            vmem(*lead, n, 2, unit, lanes),
            vmem(*lead, 2, unit, lanes),
            vmem(*lead, n, 2, unit, lanes),
            sems(*lead), sems(*lead),
            sems(*lead, n), sems(*lead, n),
            sems(*lead, n), sems(*lead, n),
        ],
        compiler_params=pltpu.CompilerParams(
            collective_id=0, has_side_effects=True, vmem_limit_bytes=16 * 1024 * 1024
        ),
    )(front_init.reshape(rows * parts, lanes), flat(green_hist), flat(field_hist))
    return result.reshape(front_init.shape)


def solution(mesh):
    in_specs = (
        P(None, None, None, "row"),
        P("row", None, None, "col"),
        P("row", None, None, "col"),
    )
    out_specs = P(None, None, None, "row")
    return jax.shard_map(
        per_device, mesh=mesh, in_specs=in_specs, out_specs=out_specs, check_vma=False
    )
```

```python
import functools

import jax
import jax.numpy as jnp
from jax import lax
from jax.experimental import pallas as pl
from jax.experimental.pallas import tpu as pltpu
from jax.sharding import PartitionSpec as P

ITERS = 2
STEP_WEIGHT = 0.5
MOST_CHUNKS = 4
VMEM_LIMIT = 54784 * 1024
MESH = pl.DeviceIdType.MESH


def split(value):
    high = value.astype(jnp.bfloat16)
    low = (value - high.astype(jnp.float32)).astype(jnp.bfloat16)
    return high, low


def swap_orbits(real_part, imag_part, orbits):
    rows, lanes = real_part.shape
    blocks = lanes // orbits
    turned = jnp.concatenate([real_part, imag_part], axis=0).T
    pieces = [turned[at * orbits:(at + 1) * orbits] for at in range(blocks)]
    block_of_lane = lax.broadcasted_iota(jnp.int32, (orbits, lanes), 1) // orbits
    step = 1
    while step < blocks:
        low_side = (block_of_lane // step) % 2 == 0
        for at in range(blocks):
            if at & step:
                continue
            first, second = pieces[at], pieces[at + step]
            pieces[at] = jnp.where(low_side, first, pltpu.roll(second, step * orbits, 1))
            pieces[at + step] = jnp.where(low_side, pltpu.roll(first, lanes - step * orbits, 1), second)
        step *= 2
    whole = jnp.concatenate(pieces, axis=0)
    return whole[:rows], whole[rows:]


def cubic_sigma(real_part, imag_part, orbits):
    other_re, other_im = swap_orbits(real_part, imag_part, orbits)
    square_re = real_part * real_part - imag_part * imag_part
    square_im = 2.0 * real_part * imag_part
    return square_re * other_re + square_im * other_im, square_im * other_re - square_re * other_im


def expected(chunks, it, at, h):
    if at == 3:
        return 8.3 * (it + 1) + 5.2 / chunks * h
    start = 8.3 * it + (5.2 if it else 2.8) / chunks * h
    return start + (0.0, 1.65, 3.85)[at]


def kernel(
    n, chunks, orbits,
    front_hbm, green_hbm, field_hbm, out_ref,
    front_ref, green_ref, field_ref, load_sem, b_high, b_low, pair_out, pair_in, own, rs_out, rs_in, total, done,
    pair_ss, pair_rs, rs_ss, rs_rs, done_ss, done_rs,
):
    row, plane = lax.axis_index("row"), lax.axis_index("col")
    chip, core = row // 2, row % 2
    rows, lanes = front_ref.shape[0] // 2, front_ref.shape[1]
    chunk_rows = rows // chunks
    unit = chunk_rows // n
    group = lanes // 2

    def at_chip(other):
        return (other * 2 + core, plane)

    sibling = (chip * 2 + 1 - core, plane)
    chips = [lax.rem(chip + d, n) for d in range(n)]
    planes = [lax.rem(plane + d, n) for d in range(n)]

    loads = [
        pltpu.make_async_copy(src, dst, load_sem.at[at])
        for at, (src, dst) in enumerate(((green_hbm, green_ref), (field_hbm, field_ref), (front_hbm, front_ref)))
    ]
    for load in loads:
        load.start()

    barrier = pltpu.get_barrier_semaphore()
    for source in [sibling] + [at_chip(chips[d]) for d in range(1, n)]:
        pl.semaphore_signal(barrier, inc=1, device_id=source, device_id_type=MESH)

    @pl.when(chip != plane)
    def _():
        for d in range(n):
            pl.semaphore_signal(barrier, inc=1, device_id=(chips[d] * 2 + core, chip), device_id_type=MESH)

    for load in loads:
        load.wait()
    depth = green_ref.shape[0] // 4

    def prepare(side):
        at = 0
        for history in (green_ref, field_ref):
            parts = []
            for part in range(2):
                halves = [history[pl.ds(2 * half + part, depth, stride=4), :] for half in range(2)]
                parts.append(jnp.where(core == side, halves[1], halves[0]))
            real_high, real_low = split(parts[0])
            imag_high, imag_low = split(parts[1])
            for store, re, im in ((b_high, real_high, imag_high), (b_low, real_low, imag_low)):
                store[side, at:at + depth, :lanes] = re
                store[side, at:at + depth, lanes:] = im
                store[side, at + depth:at + 2 * depth, :lanes] = -im
                store[side, at + depth:at + 2 * depth, lanes:] = re
            at += 2 * depth

    def remote(src, dst, send_sem, recv_sem, device):
        return pltpu.make_async_remote_copy(
            src_ref=src, dst_ref=dst, send_sem=send_sem, recv_sem=recv_sem, device_id=device, device_id_type=MESH
        )

    def pair_copy(it, h):
        return remote(pair_out.at[it, h], pair_in.at[it, h], pair_ss.at[it, h], pair_rs.at[it, h], sibling)

    def rs_copy(it, h, d):
        to = chips[d]
        return remote(rs_out.at[it, h, to], rs_in.at[it, h, d], rs_ss.at[it, h, d], rs_rs.at[it, h, d], at_chip(to))

    def done_copy(it, h, d):
        to = (plane * 2 + core, planes[d])
        return remote(total.at[it, h], done.at[it, h, chip], done_ss.at[it, h, d], done_rs.at[it, h, chip], to)

    def front(h, part):
        return front_ref[pl.ds(2 * h * chunk_rows + part, chunk_rows, stride=2), :]

    def arrived(it, h, part):
        return jnp.concatenate([done[it, h, p, part] for p in range(n)], axis=0)

    def current(it, h):
        if it == 0:
            return front(h, 0), front(h, 1)
        return tuple(front(h, part) + STEP_WEIGHT * arrived(it - 1, h, part) for part in range(2))

    def multiply(it, h):
        real_part, imag_part = current(it, h)
        sigmas = [
            cubic_sigma(real_part[at:at + group], imag_part[at:at + group], orbits)
            for at in range(0, chunk_rows, group)
        ]
        sigma_re = jnp.concatenate([s[0] for s in sigmas], axis=0)
        sigma_im = jnp.concatenate([s[1] for s in sigmas], axis=0)
        high, low = split(jnp.concatenate([sigma_re, sigma_im, real_part, imag_part], axis=1))
        both = jnp.concatenate([high, low], axis=0)
        for side, store in enumerate((pair_out.at[it], own)):
            if it == 0 and h == 0:
                prepare(side)
            upper = jnp.dot(both, b_high[side], preferred_element_type=jnp.float32)
            image = upper[:chunk_rows] + upper[chunk_rows:]
            image = image + jnp.dot(high, b_low[side], preferred_element_type=jnp.float32)
            store[h, 0] = image[:, :lanes]
            store[h, 1] = image[:, lanes:]
            if store is not own:
                if it == 0 and h == 0:
                    pl.semaphore_wait(barrier, 2 * n - 1)
                pair_copy(it, h).start()

    def add_pair(it, h):
        pair_copy(it, h).wait_recv()
        for d in list(range(1, n)) + [0]:
            to = chips[d]
            place = pl.ds(pl.multiple_of(to * unit, unit), unit)
            for part in range(2):
                rs_out[it, h, to, part] = own[h, part, place, :] + pair_in[it, h, part, place, :]
            if d:
                rs_copy(it, h, d).start()

    def add_chips(it, h):
        for d in range(1, n):
            rs_copy(it, h, d).wait_recv()
        value = rs_out[it, h, chip]
        for d in range(1, n):
            value = value + rs_in[it, h, d]
        total[it, h] = value

        for d in range(1, n):
            done_copy(it, h, d).start()

        @pl.when(chip != plane)
        def _():
            done_copy(it, h, 0).start()

        @pl.when(chip == plane)
        def _():
            done[it, h, chip] = value

    def settle(it, h):
        for d in range(1, n):
            source = chips[d]
            landed = done.at[it, h, source]
            remote(landed, landed, done_ss.at[it, h, source], done_rs.at[it, h, source], at_chip(source)).wait_recv()

        @pl.when(chip != plane)
        def _():
            landed = done.at[it, h, chip]
            remote(landed, landed, done_ss.at[it, h, chip], done_rs.at[it, h, chip], (row, chip)).wait_recv()

    def finish(it, h):
        settle(it, h)
        if it < ITERS - 1:
            multiply(it + 1, h)
        if it == ITERS - 1:
            for part in range(2):
                place = pl.ds(2 * h * chunk_rows + part, chunk_rows, stride=2)
                out_ref[place, :] = front(h, part) + STEP_WEIGHT * arrived(it, h, part)

    stages = (multiply, add_pair, add_chips, finish)
    tasks = [
        (it, at, h)
        for it in range(ITERS) for at in range(len(stages)) for h in range(chunks)
        if it == 0 or at > 0
    ]
    tasks.sort(key=lambda task: expected(chunks, *task))
    for it, at, h in tasks:
        stages[at](it, h)

    for it in range(ITERS):
        for h in range(chunks):
            pair_copy(it, h).wait_send()
            for d in range(1, n):
                rs_copy(it, h, d).wait_send()
                done_copy(it, h, d).wait_send()

            @pl.when(chip != plane)
            def _():
                done_copy(it, h, 0).wait_send()


def per_device(front_init, green_hist, field_hist):
    n = lax.axis_size("col")
    if lax.axis_size("row") != 2 * n or green_hist.shape[3] != 2 * front_init.shape[3]:
        raise ValueError("unexpected mesh")
    count, orbits, parts, lanes = front_init.shape
    rows = count * orbits
    chunks = max(1, min(MOST_CHUNKS, rows // (8 * n), 2 * rows // lanes))
    unit = rows // (chunks * n)

    def flat(history):
        steps, depth = history.shape[:2]
        return history.reshape(steps * depth, parts, 2, lanes).transpose(0, 2, 1, 3).reshape(-1, lanes)

    def vmem(*shape):
        return pltpu.VMEM(shape, jnp.float32)

    depth = green_hist.shape[0] * green_hist.shape[1]
    lead = (ITERS, chunks)
    sems = lambda *shape: pltpu.SemaphoreType.DMA(shape)
    result = pl.pallas_call(
        functools.partial(kernel, n, chunks, orbits),
        out_shape=jax.ShapeDtypeStruct((rows * parts, lanes), jnp.float32),
        in_specs=[pl.BlockSpec(memory_space=pltpu.HBM)] * 3,
        out_specs=pl.BlockSpec(memory_space=pltpu.VMEM),
        scratch_shapes=[
            vmem(rows * parts, lanes),
            vmem(4 * depth, lanes),
            vmem(4 * depth, lanes),
            sems(3),
            pltpu.VMEM((2, 4 * depth, 2 * lanes), jnp.bfloat16),
            pltpu.VMEM((2, 4 * depth, 2 * lanes), jnp.bfloat16),
            vmem(*lead, 2, rows // chunks, lanes),
            vmem(*lead, 2, rows // chunks, lanes),
            vmem(chunks, 2, rows // chunks, lanes),
            vmem(*lead, n, 2, unit, lanes),
            vmem(*lead, n, 2, unit, lanes),
            vmem(*lead, 2, unit, lanes),
            vmem(*lead, n, 2, unit, lanes),
            sems(*lead), sems(*lead),
            sems(*lead, n), sems(*lead, n),
            sems(*lead, n), sems(*lead, n),
        ],
        compiler_params=pltpu.CompilerParams(
            collective_id=0, has_side_effects=True, vmem_limit_bytes=VMEM_LIMIT
        ),
    )(front_init.reshape(rows * parts, lanes), flat(green_hist), flat(field_hist))
    return result.reshape(front_init.shape)


def solution(mesh):
    in_specs = (
        P(None, None, None, "row"),
        P("row", None, None, "col"),
        P("row", None, None, "col"),
    )
    out_specs = P(None, None, None, "row")
    return jax.shard_map(
        per_device, mesh=mesh, in_specs=in_specs, out_specs=out_specs, check_vma=False
    )
```

```python
import functools

import jax
import jax.numpy as jnp
from jax import lax
from jax.experimental import pallas as pl
from jax.experimental.pallas import tpu as pltpu
from jax.sharding import PartitionSpec as P

ITERS = 2
STEP_WEIGHT = 0.5
MOST_CHUNKS = 4
VMEM_LIMIT = 54784 * 1024
MESH = pl.DeviceIdType.MESH


def split(value):
    high = value.astype(jnp.bfloat16)
    low = (value - high.astype(jnp.float32)).astype(jnp.bfloat16)
    return high, low


def swap_orbits(real_part, imag_part, orbits):
    rows, lanes = real_part.shape
    blocks = lanes // orbits
    turned = jnp.concatenate([real_part, imag_part], axis=0).T
    pieces = [turned[at * orbits:(at + 1) * orbits] for at in range(blocks)]
    block_of_lane = lax.broadcasted_iota(jnp.int32, (orbits, lanes), 1) // orbits
    step = 1
    while step < blocks:
        low_side = (block_of_lane // step) % 2 == 0
        for at in range(blocks):
            if at & step:
                continue
            first, second = pieces[at], pieces[at + step]
            pieces[at] = jnp.where(low_side, first, pltpu.roll(second, step * orbits, 1))
            pieces[at + step] = jnp.where(low_side, pltpu.roll(first, lanes - step * orbits, 1), second)
        step *= 2
    whole = jnp.concatenate(pieces, axis=0)
    return whole[:rows], whole[rows:]


def cubic_sigma(real_part, imag_part, orbits):
    other_re, other_im = swap_orbits(real_part, imag_part, orbits)
    square_re = real_part * real_part - imag_part * imag_part
    square_im = 2.0 * real_part * imag_part
    return square_re * other_re + square_im * other_im, square_im * other_re - square_re * other_im


def expected(chunks, it, at, h):
    if at == 3:
        return 8.3 * (it + 1) + 5.2 / chunks * h
    start = 8.3 * it + (5.2 if it else 2.8) / chunks * h
    return start + (0.0, 1.65, 3.85)[at]


def kernel(
    n, chunks, orbits,
    front_hbm, green_hbm, field_hbm, out_ref,
    front_ref, green_ref, field_ref, load_sem, b_high, b_low, pair_out, pair_in, own, rs_out, rs_in, total, done,
    pair_ss, pair_rs, rs_ss, rs_rs, done_ss, done_rs,
):
    row, plane = lax.axis_index("row"), lax.axis_index("col")
    chip, core = row // 2, row % 2
    rows, lanes = front_ref.shape[0] // 2, front_ref.shape[1]
    chunk_rows = rows // chunks
    unit = chunk_rows // n
    group = lanes // 2

    def at_chip(other):
        return (other * 2 + core, plane)

    sibling = (chip * 2 + 1 - core, plane)
    chips = [lax.rem(chip + d, n) for d in range(n)]
    planes = [lax.rem(plane + d, n) for d in range(n)]

    loads = [
        pltpu.make_async_copy(src, dst, load_sem.at[at])
        for at, (src, dst) in enumerate(((green_hbm, green_ref), (field_hbm, field_ref), (front_hbm, front_ref)))
    ]
    for load in loads:
        load.start()

    barrier = pltpu.get_barrier_semaphore()
    for source in [sibling] + [at_chip(chips[d]) for d in range(1, n)]:
        pl.semaphore_signal(barrier, inc=1, device_id=source, device_id_type=MESH)

    @pl.when(chip != plane)
    def _():
        for d in range(n):
            pl.semaphore_signal(barrier, inc=1, device_id=(chips[d] * 2 + core, chip), device_id_type=MESH)

    for load in loads:
        load.wait()
    depth = green_ref.shape[0] // 4

    def prepare(side):
        at = 0
        for history in (green_ref, field_ref):
            parts = []
            for part in range(2):
                halves = [history[pl.ds(2 * half + part, depth, stride=4), :] for half in range(2)]
                parts.append(jnp.where(core == side, halves[1], halves[0]))
            real_high, real_low = split(parts[0])
            imag_high, imag_low = split(parts[1])
            for store, re, im in ((b_high, real_high, imag_high), (b_low, real_low, imag_low)):
                store[side, at:at + depth, :lanes] = re
                store[side, at:at + depth, lanes:] = im
                store[side, at + depth:at + 2 * depth, :lanes] = -im
                store[side, at + depth:at + 2 * depth, lanes:] = re
            at += 2 * depth

    def remote(src, dst, send_sem, recv_sem, device):
        return pltpu.make_async_remote_copy(
            src_ref=src, dst_ref=dst, send_sem=send_sem, recv_sem=recv_sem, device_id=device, device_id_type=MESH
        )

    def pair_copy(it, h):
        return remote(pair_out.at[it, h], pair_in.at[it, h], pair_ss.at[it, h], pair_rs.at[it, h], sibling)

    def rs_copy(it, h, d):
        return remote(rs_out.at[it, h, d], rs_in.at[it, h, d], rs_ss.at[it, h], rs_rs.at[it, h], at_chip(chips[d]))

    def rs_all(it, h):
        most = pl.ds(1, n - 1)
        return remote(rs_out.at[it, h, most], rs_in.at[it, h, most], rs_ss.at[it, h], rs_rs.at[it, h], at_chip(chips[1]))

    def done_copy(it, h, d):
        to = (plane * 2 + core, planes[d])
        return remote(total.at[it, h], done.at[it, h, chip], done_ss.at[it, h], done_rs.at[it, h], to)

    def done_all(it, h, count):
        pieces = done.at[it, h, pl.ds(0, count)]
        return remote(pieces, pieces, done_ss.at[it, h], done_rs.at[it, h], sibling)

    def wait_done(it, h, send):
        @pl.when(chip != plane)
        def _():
            copy = done_all(it, h, n)
            copy.wait_send() if send else copy.wait_recv()

        @pl.when(chip == plane)
        def _():
            copy = done_all(it, h, n - 1)
            copy.wait_send() if send else copy.wait_recv()

    def front(h, part):
        return front_ref[pl.ds(2 * h * chunk_rows + part, chunk_rows, stride=2), :]

    def arrived(it, h, part):
        return jnp.concatenate([done[it, h, p, part] for p in range(n)], axis=0)

    def current(it, h):
        if it == 0:
            return front(h, 0), front(h, 1)
        return tuple(front(h, part) + STEP_WEIGHT * arrived(it - 1, h, part) for part in range(2))

    def multiply(it, h):
        real_part, imag_part = current(it, h)
        sigmas = [
            cubic_sigma(real_part[at:at + group], imag_part[at:at + group], orbits)
            for at in range(0, chunk_rows, group)
        ]
        sigma_re = jnp.concatenate([s[0] for s in sigmas], axis=0)
        sigma_im = jnp.concatenate([s[1] for s in sigmas], axis=0)
        high, low = split(jnp.concatenate([sigma_re, sigma_im, real_part, imag_part], axis=1))
        both = jnp.concatenate([high, low], axis=0)
        for side, store in enumerate((pair_out.at[it], own)):
            if it == 0 and h == 0:
                prepare(side)
            upper = jnp.dot(both, b_high[side], preferred_element_type=jnp.float32)
            image = upper[:chunk_rows] + upper[chunk_rows:]
            image = image + jnp.dot(high, b_low[side], preferred_element_type=jnp.float32)
            store[h, 0] = image[:, :lanes]
            store[h, 1] = image[:, lanes:]
            if store is not own:
                if it == 0 and h == 0:
                    pl.semaphore_wait(barrier, 2 * n - 1)
                pair_copy(it, h).start()

    def add_pair(it, h):
        pair_copy(it, h).wait_recv()
        for d in list(range(1, n)) + [0]:
            to = chips[d]
            place = pl.ds(pl.multiple_of(to * unit, unit), unit)
            for part in range(2):
                rs_out[it, h, d, part] = own[h, part, place, :] + pair_in[it, h, part, place, :]
            if d:
                rs_copy(it, h, d).start()

    def add_chips(it, h):
        rs_all(it, h).wait_recv()
        value = rs_out[it, h, 0]
        for d in range(1, n):
            value = value + rs_in[it, h, d]
        total[it, h] = value

        for d in range(1, n):
            done_copy(it, h, d).start()

        @pl.when(chip != plane)
        def _():
            done_copy(it, h, 0).start()

        @pl.when(chip == plane)
        def _():
            done[it, h, chip] = value

    def drain():
        for it in range(ITERS):
            for h in range(chunks):
                pair_copy(it, h).wait_send()
                rs_all(it, h).wait_send()
                if it < ITERS - 1:
                    wait_done(it, h, True)

    def finish(it, h):
        if it == ITERS - 1 and h == 0:
            drain()
        wait_done(it, h, False)
        if it < ITERS - 1:
            multiply(it + 1, h)
        if it == ITERS - 1:
            for part in range(2):
                place = pl.ds(2 * h * chunk_rows + part, chunk_rows, stride=2)
                out_ref[place, :] = front(h, part) + STEP_WEIGHT * arrived(it, h, part)

    stages = (multiply, add_pair, add_chips, finish)
    tasks = [
        (it, at, h)
        for it in range(ITERS) for at in range(len(stages)) for h in range(chunks)
        if it == 0 or at > 0
    ]
    tasks.sort(key=lambda task: expected(chunks, *task))
    for it, at, h in tasks:
        stages[at](it, h)

    for h in range(chunks):
        wait_done(ITERS - 1, h, True)


def per_device(front_init, green_hist, field_hist):
    n = lax.axis_size("col")
    if lax.axis_size("row") != 2 * n or green_hist.shape[3] != 2 * front_init.shape[3]:
        raise ValueError("unexpected mesh")
    count, orbits, parts, lanes = front_init.shape
    rows = count * orbits
    chunks = max(1, min(MOST_CHUNKS, rows // (8 * n), 2 * rows // lanes))
    unit = rows // (chunks * n)

    def flat(history):
        steps, depth = history.shape[:2]
        return history.reshape(steps * depth, parts, 2, lanes).transpose(0, 2, 1, 3).reshape(-1, lanes)

    def vmem(*shape):
        return pltpu.VMEM(shape, jnp.float32)

    depth = green_hist.shape[0] * green_hist.shape[1]
    lead = (ITERS, chunks)
    sems = lambda *shape: pltpu.SemaphoreType.DMA(shape)
    result = pl.pallas_call(
        functools.partial(kernel, n, chunks, orbits),
        out_shape=jax.ShapeDtypeStruct((rows * parts, lanes), jnp.float32),
        in_specs=[pl.BlockSpec(memory_space=pltpu.HBM)] * 3,
        out_specs=pl.BlockSpec(memory_space=pltpu.VMEM),
        scratch_shapes=[
            vmem(rows * parts, lanes),
            vmem(4 * depth, lanes),
            vmem(4 * depth, lanes),
            sems(3),
            pltpu.VMEM((2, 4 * depth, 2 * lanes), jnp.bfloat16),
            pltpu.VMEM((2, 4 * depth, 2 * lanes), jnp.bfloat16),
            vmem(*lead, 2, rows // chunks, lanes),
            vmem(*lead, 2, rows // chunks, lanes),
            vmem(chunks, 2, rows // chunks, lanes),
            vmem(*lead, n, 2, unit, lanes),
            vmem(*lead, n, 2, unit, lanes),
            vmem(*lead, 2, unit, lanes),
            vmem(*lead, n, 2, unit, lanes),
            sems(*lead), sems(*lead),
            sems(*lead), sems(*lead),
            sems(*lead), sems(*lead),
        ],
        compiler_params=pltpu.CompilerParams(
            collective_id=0, has_side_effects=True, vmem_limit_bytes=VMEM_LIMIT
        ),
    )(front_init.reshape(rows * parts, lanes), flat(green_hist), flat(field_hist))
    return result.reshape(front_init.shape)


def solution(mesh):
    in_specs = (
        P(None, None, None, "row"),
        P("row", None, None, "col"),
        P("row", None, None, "col"),
    )
    out_specs = P(None, None, None, "row")
    return jax.shard_map(
        per_device, mesh=mesh, in_specs=in_specs, out_specs=out_specs, check_vma=False
    )
```

```python
import functools

import jax
import jax.numpy as jnp
from jax import lax
from jax.experimental import pallas as pl
from jax.experimental.pallas import tpu as pltpu
from jax.sharding import PartitionSpec as P

ITERS = 2
STEP_WEIGHT = 0.5
MOST_CHUNKS = 4
VMEM_LIMIT = 54784 * 1024
MESH = pl.DeviceIdType.MESH


def split(value):
    high = value.astype(jnp.bfloat16)
    low = (value - high.astype(jnp.float32)).astype(jnp.bfloat16)
    return high, low


def swap_orbits(real_part, imag_part, orbits):
    rows, lanes = real_part.shape
    blocks = lanes // orbits
    turned = jnp.concatenate([real_part, imag_part], axis=0).T
    pieces = [turned[at * orbits:(at + 1) * orbits] for at in range(blocks)]
    block_of_lane = lax.broadcasted_iota(jnp.int32, (orbits, lanes), 1) // orbits
    step = 1
    while step < blocks:
        low_side = (block_of_lane // step) % 2 == 0
        for at in range(blocks):
            if at & step:
                continue
            first, second = pieces[at], pieces[at + step]
            pieces[at] = jnp.where(low_side, first, pltpu.roll(second, step * orbits, 1))
            pieces[at + step] = jnp.where(low_side, pltpu.roll(first, lanes - step * orbits, 1), second)
        step *= 2
    whole = jnp.concatenate(pieces, axis=0)
    return whole[:rows], whole[rows:]


def cubic_sigma(real_part, imag_part, orbits):
    other_re, other_im = swap_orbits(real_part, imag_part, orbits)
    square_re = real_part * real_part - imag_part * imag_part
    square_im = 2.0 * real_part * imag_part
    return square_re * other_re + square_im * other_im, square_im * other_re - square_re * other_im


def expected(chunks, it, at, h):
    if at == 3:
        return 8.3 * (it + 1) + 5.2 / chunks * h
    start = 8.3 * it + (5.2 if it else 2.8) / chunks * h
    return start + ((0.0, 1.65, 3.85) if it else (0.0, 1.3, 3.3))[at]


def kernel(
    n, chunks, orbits,
    front_hbm, green_hbm, field_hbm, out_ref,
    front_ref, green_ref, field_ref, load_sem, b_high, b_low, pair_out, pair_in, own, rs_out, rs_in, total, done,
    pair_ss, pair_rs, rs_ss, rs_rs, done_ss, done_rs,
):
    row, plane = lax.axis_index("row"), lax.axis_index("col")
    chip, core = row // 2, row % 2
    rows, lanes = front_ref.shape[0] // 2, front_ref.shape[1]
    chunk_rows = rows // chunks
    unit = chunk_rows // n
    group = lanes // 2

    def at_chip(other):
        return (other * 2 + core, plane)

    sibling = (chip * 2 + 1 - core, plane)
    chips = [lax.rem(chip + d, n) for d in range(n)]
    planes = [lax.rem(plane + d, n) for d in range(n)]

    loads = [
        pltpu.make_async_copy(src, dst, load_sem.at[at])
        for at, (src, dst) in enumerate(((green_hbm, green_ref), (field_hbm, field_ref), (front_hbm, front_ref)))
    ]
    for load in loads:
        load.start()

    barrier = pltpu.get_barrier_semaphore()
    for source in [sibling] + [at_chip(chips[d]) for d in range(1, n)]:
        pl.semaphore_signal(barrier, inc=1, device_id=source, device_id_type=MESH)

    @pl.when(chip != plane)
    def _():
        for d in range(n):
            pl.semaphore_signal(barrier, inc=1, device_id=(chips[d] * 2 + core, chip), device_id_type=MESH)

    for load in loads:
        load.wait()
    depth = green_ref.shape[0] // 4

    def prepare(side):
        at = 0
        for history in (green_ref, field_ref):
            parts = []
            for part in range(2):
                halves = [history[pl.ds(2 * half + part, depth, stride=4), :] for half in range(2)]
                parts.append(jnp.where(core == side, halves[1], halves[0]))
            real_high, real_low = split(parts[0])
            imag_high, imag_low = split(parts[1])
            for store, re, im in ((b_high, real_high, imag_high), (b_low, real_low, imag_low)):
                store[side, at:at + depth, :lanes] = re
                store[side, at:at + depth, lanes:] = im
                store[side, at + depth:at + 2 * depth, :lanes] = -im
                store[side, at + depth:at + 2 * depth, lanes:] = re
            at += 2 * depth

    def remote(src, dst, send_sem, recv_sem, device):
        return pltpu.make_async_remote_copy(
            src_ref=src, dst_ref=dst, send_sem=send_sem, recv_sem=recv_sem, device_id=device, device_id_type=MESH
        )

    def pair_copy(it, h):
        return remote(pair_out.at[it, h], pair_in.at[it, h], pair_ss.at[it, h], pair_rs.at[it, h], sibling)

    def rs_copy(it, h, d):
        return remote(rs_out.at[it, h, d], rs_in.at[it, h, d], rs_ss.at[it, h], rs_rs.at[it, h], at_chip(chips[d]))

    def rs_all(it, h):
        most = pl.ds(1, n - 1)
        return remote(rs_out.at[it, h, most], rs_in.at[it, h, most], rs_ss.at[it, h], rs_rs.at[it, h], at_chip(chips[1]))

    def done_copy(it, h, d):
        to = (plane * 2 + core, planes[d])
        return remote(total.at[it, h], done.at[it, h, chip], done_ss.at[it, h], done_rs.at[it, h], to)

    def done_all(it, h, count):
        pieces = done.at[it, h, pl.ds(0, count)]
        return remote(pieces, pieces, done_ss.at[it, h], done_rs.at[it, h], sibling)

    def wait_done(it, h, send):
        @pl.when(chip != plane)
        def _():
            copy = done_all(it, h, n)
            copy.wait_send() if send else copy.wait_recv()

        @pl.when(chip == plane)
        def _():
            copy = done_all(it, h, n - 1)
            copy.wait_send() if send else copy.wait_recv()

    def front(h, part):
        return front_ref[pl.ds(2 * h * chunk_rows + part, chunk_rows, stride=2), :]

    def arrived(it, h, part):
        return jnp.concatenate([done[it, h, p, part] for p in range(n)], axis=0)

    def current(it, h):
        if it == 0:
            return front(h, 0), front(h, 1)
        return tuple(front(h, part) + STEP_WEIGHT * arrived(it - 1, h, part) for part in range(2))

    def multiply(it, h):
        real_part, imag_part = current(it, h)
        sigmas = [
            cubic_sigma(real_part[at:at + group], imag_part[at:at + group], orbits)
            for at in range(0, chunk_rows, group)
        ]
        sigma_re = jnp.concatenate([s[0] for s in sigmas], axis=0)
        sigma_im = jnp.concatenate([s[1] for s in sigmas], axis=0)
        high, low = split(jnp.concatenate([sigma_re, sigma_im, real_part, imag_part], axis=1))
        both = jnp.concatenate([high, low], axis=0)
        for side, store in enumerate((pair_out.at[it], own)):
            if it == 0 and h == 0:
                prepare(side)
            upper = jnp.dot(both, b_high[side], preferred_element_type=jnp.float32)
            image = upper[:chunk_rows] + upper[chunk_rows:]
            image = image + jnp.dot(high, b_low[side], preferred_element_type=jnp.float32)
            store[h, 0] = image[:, :lanes]
            store[h, 1] = image[:, lanes:]
            if store is not own:
                if it == 0 and h == 0:
                    pl.semaphore_wait(barrier, 2 * n - 1)
                pair_copy(it, h).start()

    def add_pair(it, h):
        pair_copy(it, h).wait_recv()
        for d in list(range(1, n)) + [0]:
            to = chips[d]
            place = pl.ds(pl.multiple_of(to * unit, unit), unit)
            for part in range(2):
                rs_out[it, h, d, part] = own[h, part, place, :] + pair_in[it, h, part, place, :]
            if d:
                rs_copy(it, h, d).start()

    def add_chips(it, h):
        rs_all(it, h).wait_recv()
        value = rs_out[it, h, 0]
        for d in range(1, n):
            value = value + rs_in[it, h, d]
        total[it, h] = value

        for d in range(1, n):
            done_copy(it, h, d).start()

        @pl.when(chip != plane)
        def _():
            done_copy(it, h, 0).start()

        @pl.when(chip == plane)
        def _():
            done[it, h, chip] = value

    def drain():
        for it in range(ITERS):
            for h in range(chunks):
                pair_copy(it, h).wait_send()
                rs_all(it, h).wait_send()
                if it < ITERS - 1:
                    wait_done(it, h, True)

    def finish(it, h):
        if it == ITERS - 1 and h == 0:
            drain()
        wait_done(it, h, False)
        if it < ITERS - 1:
            multiply(it + 1, h)
        if it == ITERS - 1:
            for part in range(2):
                place = pl.ds(2 * h * chunk_rows + part, chunk_rows, stride=2)
                out_ref[place, :] = front(h, part) + STEP_WEIGHT * arrived(it, h, part)

    stages = (multiply, add_pair, add_chips, finish)
    tasks = [
        (it, at, h)
        for it in range(ITERS) for at in range(len(stages)) for h in range(chunks)
        if it == 0 or at > 0
    ]
    tasks.sort(key=lambda task: expected(chunks, *task))
    for it, at, h in tasks:
        stages[at](it, h)

    for h in range(chunks):
        wait_done(ITERS - 1, h, True)


def per_device(front_init, green_hist, field_hist):
    n = lax.axis_size("col")
    if lax.axis_size("row") != 2 * n or green_hist.shape[3] != 2 * front_init.shape[3]:
        raise ValueError("unexpected mesh")
    count, orbits, parts, lanes = front_init.shape
    rows = count * orbits
    chunks = max(1, min(MOST_CHUNKS, rows // (8 * n), 2 * rows // lanes))
    unit = rows // (chunks * n)

    def flat(history):
        steps, depth = history.shape[:2]
        return history.reshape(steps * depth, parts, 2, lanes).transpose(0, 2, 1, 3).reshape(-1, lanes)

    def vmem(*shape):
        return pltpu.VMEM(shape, jnp.float32)

    depth = green_hist.shape[0] * green_hist.shape[1]
    lead = (ITERS, chunks)
    sems = lambda *shape: pltpu.SemaphoreType.DMA(shape)
    result = pl.pallas_call(
        functools.partial(kernel, n, chunks, orbits),
        out_shape=jax.ShapeDtypeStruct((rows * parts, lanes), jnp.float32),
        in_specs=[pl.BlockSpec(memory_space=pltpu.HBM)] * 3,
        out_specs=pl.BlockSpec(memory_space=pltpu.VMEM),
        scratch_shapes=[
            vmem(rows * parts, lanes),
            vmem(4 * depth, lanes),
            vmem(4 * depth, lanes),
            sems(3),
            pltpu.VMEM((2, 4 * depth, 2 * lanes), jnp.bfloat16),
            pltpu.VMEM((2, 4 * depth, 2 * lanes), jnp.bfloat16),
            vmem(*lead, 2, rows // chunks, lanes),
            vmem(*lead, 2, rows // chunks, lanes),
            vmem(chunks, 2, rows // chunks, lanes),
            vmem(*lead, n, 2, unit, lanes),
            vmem(*lead, n, 2, unit, lanes),
            vmem(*lead, 2, unit, lanes),
            vmem(*lead, n, 2, unit, lanes),
            sems(*lead), sems(*lead),
            sems(*lead), sems(*lead),
            sems(*lead), sems(*lead),
        ],
        compiler_params=pltpu.CompilerParams(
            collective_id=0, has_side_effects=True, vmem_limit_bytes=VMEM_LIMIT
        ),
    )(front_init.reshape(rows * parts, lanes), flat(green_hist), flat(field_hist))
    return result.reshape(front_init.shape)


def solution(mesh):
    in_specs = (
        P(None, None, None, "row"),
        P("row", None, None, "col"),
        P("row", None, None, "col"),
    )
    out_specs = P(None, None, None, "row")
    return jax.shard_map(
        per_device, mesh=mesh, in_specs=in_specs, out_specs=out_specs, check_vma=False
    )
```

```python
import functools

import jax
import jax.numpy as jnp
from jax import lax
from jax.experimental import pallas as pl
from jax.experimental.pallas import tpu as pltpu
from jax.sharding import PartitionSpec as P

ITERS = 2
STEP_WEIGHT = 0.5
MOST_CHUNKS = 2
VMEM_LIMIT = 54784 * 1024
MESH = pl.DeviceIdType.MESH


def split(value):
    high = value.astype(jnp.bfloat16)
    low = (value - high.astype(jnp.float32)).astype(jnp.bfloat16)
    return high, low


def swap_orbits(real_part, imag_part, orbits):
    rows, lanes = real_part.shape
    blocks = lanes // orbits
    turned = jnp.concatenate([real_part, imag_part], axis=0).T
    pieces = [turned[at * orbits:(at + 1) * orbits] for at in range(blocks)]
    block_of_lane = lax.broadcasted_iota(jnp.int32, (orbits, lanes), 1) // orbits
    step = 1
    while step < blocks:
        low_side = (block_of_lane // step) % 2 == 0
        for at in range(blocks):
            if at & step:
                continue
            first, second = pieces[at], pieces[at + step]
            pieces[at] = jnp.where(low_side, first, pltpu.roll(second, step * orbits, 1))
            pieces[at + step] = jnp.where(low_side, pltpu.roll(first, lanes - step * orbits, 1), second)
        step *= 2
    whole = jnp.concatenate(pieces, axis=0)
    return whole[:rows], whole[rows:]


def cubic_sigma(real_part, imag_part, orbits):
    other_re, other_im = swap_orbits(real_part, imag_part, orbits)
    square_re = real_part * real_part - imag_part * imag_part
    square_im = 2.0 * real_part * imag_part
    return square_re * other_re + square_im * other_im, square_im * other_re - square_re * other_im


def expected(chunks, it, at, h):
    if at == 3:
        return 8.3 * (it + 1) + 5.2 / chunks * h
    start = 8.3 * it + (5.2 if it else 2.8) / chunks * h
    return start + ((0.0, 1.65, 3.85) if it else (0.0, 1.3, 3.3))[at]


def kernel(
    n, chunks, orbits,
    front_hbm, green_hbm, field_hbm, out_ref,
    front_ref, green_ref, field_ref, load_sem, b_high, b_low, pair_out, pair_in, own, rs_out, rs_in, total, done,
    pair_ss, pair_rs, rs_ss, rs_rs, done_ss, done_rs,
):
    row, plane = lax.axis_index("row"), lax.axis_index("col")
    chip, core = row // 2, row % 2
    rows, lanes = front_ref.shape[0] // 2, front_ref.shape[1]
    chunk_rows = rows // chunks
    unit = chunk_rows // n
    group = lanes // 2

    def at_chip(other):
        return (other * 2 + core, plane)

    sibling = (chip * 2 + 1 - core, plane)
    chips = [lax.rem(chip + d, n) for d in range(n)]
    planes = [lax.rem(plane + d, n) for d in range(n)]

    loads = [
        pltpu.make_async_copy(src, dst, load_sem.at[at])
        for at, (src, dst) in enumerate(((green_hbm, green_ref), (field_hbm, field_ref), (front_hbm, front_ref)))
    ]
    for load in loads:
        load.start()

    barrier = pltpu.get_barrier_semaphore()
    for source in [sibling] + [at_chip(chips[d]) for d in range(1, n)]:
        pl.semaphore_signal(barrier, inc=1, device_id=source, device_id_type=MESH)

    @pl.when(chip != plane)
    def _():
        for d in range(n):
            pl.semaphore_signal(barrier, inc=1, device_id=(chips[d] * 2 + core, chip), device_id_type=MESH)

    for load in loads:
        load.wait()
    depth = green_ref.shape[0] // 4

    def prepare(side):
        at = 0
        for history in (green_ref, field_ref):
            parts = []
            for part in range(2):
                halves = [history[pl.ds(2 * half + part, depth, stride=4), :] for half in range(2)]
                parts.append(jnp.where(core == side, halves[1], halves[0]))
            real_high, real_low = split(parts[0])
            imag_high, imag_low = split(parts[1])
            for store, re, im in ((b_high, real_high, imag_high), (b_low, real_low, imag_low)):
                store[side, at:at + depth, :lanes] = re
                store[side, at:at + depth, lanes:] = im
                store[side, at + depth:at + 2 * depth, :lanes] = -im
                store[side, at + depth:at + 2 * depth, lanes:] = re
            at += 2 * depth

    def remote(src, dst, send_sem, recv_sem, device):
        return pltpu.make_async_remote_copy(
            src_ref=src, dst_ref=dst, send_sem=send_sem, recv_sem=recv_sem, device_id=device, device_id_type=MESH
        )

    def pair_copy(it, h):
        return remote(pair_out.at[it, h], pair_in.at[it, h], pair_ss.at[it, h], pair_rs.at[it, h], sibling)

    def rs_copy(it, h, d):
        return remote(rs_out.at[it, h, d], rs_in.at[it, h, d], rs_ss.at[it, h], rs_rs.at[it, h], at_chip(chips[d]))

    def rs_all(it, h):
        most = pl.ds(1, n - 1)
        return remote(rs_out.at[it, h, most], rs_in.at[it, h, most], rs_ss.at[it, h], rs_rs.at[it, h], at_chip(chips[1]))

    def done_copy(it, h, d):
        to = (plane * 2 + core, planes[d])
        return remote(total.at[it, h], done.at[it, h, chip], done_ss.at[it, h], done_rs.at[it, h], to)

    def done_all(it, h, count):
        pieces = done.at[it, h, pl.ds(0, count)]
        return remote(pieces, pieces, done_ss.at[it, h], done_rs.at[it, h], sibling)

    def wait_done(it, h, send):
        @pl.when(chip != plane)
        def _():
            copy = done_all(it, h, n)
            copy.wait_send() if send else copy.wait_recv()

        @pl.when(chip == plane)
        def _():
            copy = done_all(it, h, n - 1)
            copy.wait_send() if send else copy.wait_recv()

    def front(h, part):
        return front_ref[pl.ds(2 * h * chunk_rows + part, chunk_rows, stride=2), :]

    def arrived(it, h, part):
        return jnp.concatenate([done[it, h, p, part] for p in range(n)], axis=0)

    def current(it, h):
        if it == 0:
            return front(h, 0), front(h, 1)
        return tuple(front(h, part) + STEP_WEIGHT * arrived(it - 1, h, part) for part in range(2))

    def multiply(it, h):
        real_part, imag_part = current(it, h)
        sigmas = [
            cubic_sigma(real_part[at:at + group], imag_part[at:at + group], orbits)
            for at in range(0, chunk_rows, group)
        ]
        sigma_re = jnp.concatenate([s[0] for s in sigmas], axis=0)
        sigma_im = jnp.concatenate([s[1] for s in sigmas], axis=0)
        high, low = split(jnp.concatenate([sigma_re, sigma_im, real_part, imag_part], axis=1))
        both = jnp.concatenate([high, low], axis=0)
        for side, store in enumerate((pair_out.at[it], own)):
            if it == 0 and h == 0:
                prepare(side)
            upper = jnp.dot(both, b_high[side], preferred_element_type=jnp.float32)
            image = upper[:chunk_rows] + upper[chunk_rows:]
            image = image + jnp.dot(high, b_low[side], preferred_element_type=jnp.float32)
            store[h, 0] = image[:, :lanes]
            store[h, 1] = image[:, lanes:]
            if store is not own:
                if it == 0 and h == 0:
                    pl.semaphore_wait(barrier, 2 * n - 1)
                pair_copy(it, h).start()

    def add_pair(it, h):
        pair_copy(it, h).wait_recv()
        for d in list(range(1, n)) + [0]:
            to = chips[d]
            place = pl.ds(pl.multiple_of(to * unit, unit), unit)
            for part in range(2):
                rs_out[it, h, d, part] = own[h, part, place, :] + pair_in[it, h, part, place, :]
            if d:
                rs_copy(it, h, d).start()

    def add_chips(it, h):
        rs_all(it, h).wait_recv()
        value = rs_out[it, h, 0]
        for d in range(1, n):
            value = value + rs_in[it, h, d]
        total[it, h] = value

        for d in range(1, n):
            done_copy(it, h, d).start()

        @pl.when(chip != plane)
        def _():
            done_copy(it, h, 0).start()

        @pl.when(chip == plane)
        def _():
            done[it, h, chip] = value

    def drain():
        for it in range(ITERS):
            for h in range(chunks):
                pair_copy(it, h).wait_send()
                rs_all(it, h).wait_send()
                if it < ITERS - 1:
                    wait_done(it, h, True)

    def finish(it, h):
        if it == ITERS - 1 and h == 0:
            drain()
        wait_done(it, h, False)
        if it < ITERS - 1:
            multiply(it + 1, h)
        if it == ITERS - 1:
            for part in range(2):
                place = pl.ds(2 * h * chunk_rows + part, chunk_rows, stride=2)
                out_ref[place, :] = front(h, part) + STEP_WEIGHT * arrived(it, h, part)

    stages = (multiply, add_pair, add_chips, finish)
    tasks = [
        (it, at, h)
        for it in range(ITERS) for at in range(len(stages)) for h in range(chunks)
        if it == 0 or at > 0
    ]
    tasks.sort(key=lambda task: expected(chunks, *task))
    for it, at, h in tasks:
        stages[at](it, h)

    for h in range(chunks):
        wait_done(ITERS - 1, h, True)


def per_device(front_init, green_hist, field_hist):
    n = lax.axis_size("col")
    if lax.axis_size("row") != 2 * n or green_hist.shape[3] != 2 * front_init.shape[3]:
        raise ValueError("unexpected mesh")
    count, orbits, parts, lanes = front_init.shape
    rows = count * orbits
    chunks = max(1, min(MOST_CHUNKS, rows // (8 * n), 2 * rows // lanes))
    unit = rows // (chunks * n)

    def flat(history):
        steps, depth = history.shape[:2]
        return history.reshape(steps * depth, parts, 2, lanes).transpose(0, 2, 1, 3).reshape(-1, lanes)

    def vmem(*shape):
        return pltpu.VMEM(shape, jnp.float32)

    depth = green_hist.shape[0] * green_hist.shape[1]
    lead = (ITERS, chunks)
    sems = lambda *shape: pltpu.SemaphoreType.DMA(shape)
    result = pl.pallas_call(
        functools.partial(kernel, n, chunks, orbits),
        out_shape=jax.ShapeDtypeStruct((rows * parts, lanes), jnp.float32),
        in_specs=[pl.BlockSpec(memory_space=pltpu.HBM)] * 3,
        out_specs=pl.BlockSpec(memory_space=pltpu.VMEM),
        scratch_shapes=[
            vmem(rows * parts, lanes),
            vmem(4 * depth, lanes),
            vmem(4 * depth, lanes),
            sems(3),
            pltpu.VMEM((2, 4 * depth, 2 * lanes), jnp.bfloat16),
            pltpu.VMEM((2, 4 * depth, 2 * lanes), jnp.bfloat16),
            vmem(*lead, 2, rows // chunks, lanes),
            vmem(*lead, 2, rows // chunks, lanes),
            vmem(chunks, 2, rows // chunks, lanes),
            vmem(*lead, n, 2, unit, lanes),
            vmem(*lead, n, 2, unit, lanes),
            vmem(*lead, 2, unit, lanes),
            vmem(*lead, n, 2, unit, lanes),
            sems(*lead), sems(*lead),
            sems(*lead), sems(*lead),
            sems(*lead), sems(*lead),
        ],
        compiler_params=pltpu.CompilerParams(
            collective_id=0, has_side_effects=True, vmem_limit_bytes=VMEM_LIMIT
        ),
    )(front_init.reshape(rows * parts, lanes), flat(green_hist), flat(field_hist))
    return result.reshape(front_init.shape)


def solution(mesh):
    in_specs = (
        P(None, None, None, "row"),
        P("row", None, None, "col"),
        P("row", None, None, "col"),
    )
    out_specs = P(None, None, None, "row")
    return jax.shard_map(
        per_device, mesh=mesh, in_specs=in_specs, out_specs=out_specs, check_vma=False
    )
```

```python
import functools

import jax
import jax.numpy as jnp
from jax import lax
from jax.experimental import pallas as pl
from jax.experimental.pallas import tpu as pltpu
from jax.sharding import PartitionSpec as P

ITERS = 2
STEP_WEIGHT = 0.5
MOST_CHUNKS = 4
VMEM_LIMIT = 54784 * 1024
MESH = pl.DeviceIdType.MESH


def split(value):
    high = value.astype(jnp.bfloat16)
    low = (value - high.astype(jnp.float32)).astype(jnp.bfloat16)
    return high, low


def swap_orbits(real_part, imag_part, orbits):
    rows, lanes = real_part.shape
    blocks = lanes // orbits
    turned = jnp.concatenate([real_part, imag_part], axis=0).T
    pieces = [turned[at * orbits:(at + 1) * orbits] for at in range(blocks)]
    block_of_lane = lax.broadcasted_iota(jnp.int32, (orbits, lanes), 1) // orbits
    step = 1
    while step < blocks:
        low_side = (block_of_lane // step) % 2 == 0
        for at in range(blocks):
            if at & step:
                continue
            first, second = pieces[at], pieces[at + step]
            pieces[at] = jnp.where(low_side, first, pltpu.roll(second, step * orbits, 1))
            pieces[at + step] = jnp.where(low_side, pltpu.roll(first, lanes - step * orbits, 1), second)
        step *= 2
    whole = jnp.concatenate(pieces, axis=0)
    return whole[:rows], whole[rows:]


def cubic_sigma(real_part, imag_part, orbits):
    other_re, other_im = swap_orbits(real_part, imag_part, orbits)
    square_re = real_part * real_part - imag_part * imag_part
    square_im = 2.0 * real_part * imag_part
    return square_re * other_re + square_im * other_im, square_im * other_re - square_re * other_im


def expected(chunks, it, at, h):
    if at == 3:
        return 8.3 * (it + 1) + 5.2 / chunks * h
    start = 8.3 * it + (5.2 if it else 2.8) / chunks * h
    return start + ((0.0, 1.25, 3.5) if it else (0.0, 1.3, 3.3))[at]


def kernel(
    n, chunks, orbits,
    front_hbm, green_hbm, field_hbm, out_ref,
    front_ref, green_ref, field_ref, load_sem, b_high, b_low, pair_out, pair_in, own, rs_out, rs_in, total, done,
    pair_ss, pair_rs, rs_ss, rs_rs, done_ss, done_rs,
):
    row, plane = lax.axis_index("row"), lax.axis_index("col")
    chip, core = row // 2, row % 2
    rows, lanes = front_ref.shape[0] // 2, front_ref.shape[1]
    chunk_rows = rows // chunks
    unit = chunk_rows // n
    group = lanes // 2

    def at_chip(other):
        return (other * 2 + core, plane)

    sibling = (chip * 2 + 1 - core, plane)
    chips = [lax.rem(chip + d, n) for d in range(n)]
    planes = [lax.rem(plane + d, n) for d in range(n)]

    loads = [
        pltpu.make_async_copy(src, dst, load_sem.at[at])
        for at, (src, dst) in enumerate(((green_hbm, green_ref), (field_hbm, field_ref), (front_hbm, front_ref)))
    ]
    for load in loads:
        load.start()

    barrier = pltpu.get_barrier_semaphore()
    for source in [sibling] + [at_chip(chips[d]) for d in range(1, n)]:
        pl.semaphore_signal(barrier, inc=1, device_id=source, device_id_type=MESH)

    @pl.when(chip != plane)
    def _():
        for d in range(n):
            pl.semaphore_signal(barrier, inc=1, device_id=(chips[d] * 2 + core, chip), device_id_type=MESH)

    for load in loads:
        load.wait()
    depth = green_ref.shape[0] // 4

    def prepare(side):
        at = 0
        for history in (green_ref, field_ref):
            parts = []
            for part in range(2):
                halves = [history[pl.ds(2 * half + part, depth, stride=4), :] for half in range(2)]
                parts.append(jnp.where(core == side, halves[1], halves[0]))
            real_high, real_low = split(parts[0])
            imag_high, imag_low = split(parts[1])
            for store, re, im in ((b_high, real_high, imag_high), (b_low, real_low, imag_low)):
                store[side, at:at + depth, :lanes] = re
                store[side, at:at + depth, lanes:] = im
                store[side, at + depth:at + 2 * depth, :lanes] = -im
                store[side, at + depth:at + 2 * depth, lanes:] = re
            at += 2 * depth

    def remote(src, dst, send_sem, recv_sem, device):
        return pltpu.make_async_remote_copy(
            src_ref=src, dst_ref=dst, send_sem=send_sem, recv_sem=recv_sem, device_id=device, device_id_type=MESH
        )

    def pair_copy(it, h):
        return remote(pair_out.at[it, h], pair_in.at[it, h], pair_ss.at[it, h], pair_rs.at[it, h], sibling)

    def rs_copy(it, h, d):
        return remote(rs_out.at[it, h, d], rs_in.at[it, h, d], rs_ss.at[it, h], rs_rs.at[it, h], at_chip(chips[d]))

    def rs_all(it, h):
        most = pl.ds(1, n - 1)
        return remote(rs_out.at[it, h, most], rs_in.at[it, h, most], rs_ss.at[it, h], rs_rs.at[it, h], at_chip(chips[1]))

    def done_copy(it, h, d):
        to = (plane * 2 + core, planes[d])
        return remote(total.at[it, h], done.at[it, h, chip], done_ss.at[it, h], done_rs.at[it, h], to)

    def done_all(it, h, count):
        pieces = done.at[it, h, pl.ds(0, count)]
        return remote(pieces, pieces, done_ss.at[it, h], done_rs.at[it, h], sibling)

    def wait_done(it, h, send):
        @pl.when(chip != plane)
        def _():
            copy = done_all(it, h, n)
            copy.wait_send() if send else copy.wait_recv()

        @pl.when(chip == plane)
        def _():
            copy = done_all(it, h, n - 1)
            copy.wait_send() if send else copy.wait_recv()

    def front(h, part):
        return front_ref[pl.ds(2 * h * chunk_rows + part, chunk_rows, stride=2), :]

    def arrived(it, h, part):
        return jnp.concatenate([done[it, h, p, part] for p in range(n)], axis=0)

    def current(it, h):
        if it == 0:
            return front(h, 0), front(h, 1)
        return tuple(front(h, part) + STEP_WEIGHT * arrived(it - 1, h, part) for part in range(2))

    def multiply(it, h):
        real_part, imag_part = current(it, h)
        sigmas = [
            cubic_sigma(real_part[at:at + group], imag_part[at:at + group], orbits)
            for at in range(0, chunk_rows, group)
        ]
        sigma_re = jnp.concatenate([s[0] for s in sigmas], axis=0)
        sigma_im = jnp.concatenate([s[1] for s in sigmas], axis=0)
        high, low = split(jnp.concatenate([sigma_re, sigma_im, real_part, imag_part], axis=1))
        both = jnp.concatenate([high, low], axis=0)
        for side, store in enumerate((pair_out.at[it], own)):
            if it == 0 and h == 0:
                prepare(side)
            upper = jnp.dot(both, b_high[side], preferred_element_type=jnp.float32)
            image = upper[:chunk_rows] + upper[chunk_rows:]
            image = image + jnp.dot(high, b_low[side], preferred_element_type=jnp.float32)
            store[h, 0] = image[:, :lanes]
            store[h, 1] = image[:, lanes:]
            if store is not own:
                if it == 0 and h == 0:
                    pl.semaphore_wait(barrier, 2 * n - 1)
                pair_copy(it, h).start()

    def add_pair(it, h):
        pair_copy(it, h).wait_recv()
        for d in list(range(1, n)) + [0]:
            to = chips[d]
            place = pl.ds(pl.multiple_of(to * unit, unit), unit)
            for part in range(2):
                rs_out[it, h, d, part] = own[h, part, place, :] + pair_in[it, h, part, place, :]
            if d:
                rs_copy(it, h, d).start()

    def add_chips(it, h):
        rs_all(it, h).wait_recv()
        value = rs_out[it, h, 0]
        for d in range(1, n):
            value = value + rs_in[it, h, d]
        total[it, h] = value

        for d in sorted(range(1, n), key=lambda d: abs(2 * d - n)):
            done_copy(it, h, d).start()

        @pl.when(chip != plane)
        def _():
            done_copy(it, h, 0).start()

        @pl.when(chip == plane)
        def _():
            done[it, h, chip] = value

    def drain():
        for it in range(ITERS):
            for h in range(chunks):
                pair_copy(it, h).wait_send()
                rs_all(it, h).wait_send()
                if it < ITERS - 1:
                    wait_done(it, h, True)

    def finish(it, h):
        if it == ITERS - 1 and h == 0:
            drain()
        wait_done(it, h, False)
        if it < ITERS - 1:
            multiply(it + 1, h)
        if it == ITERS - 1:
            for part in range(2):
                place = pl.ds(2 * h * chunk_rows + part, chunk_rows, stride=2)
                out_ref[place, :] = front(h, part) + STEP_WEIGHT * arrived(it, h, part)

    stages = (multiply, add_pair, add_chips, finish)
    tasks = [
        (it, at, h)
        for it in range(ITERS) for at in range(len(stages)) for h in range(chunks)
        if it == 0 or at > 0
    ]
    tasks.sort(key=lambda task: expected(chunks, *task))
    for it, at, h in tasks:
        stages[at](it, h)

    for h in range(chunks):
        wait_done(ITERS - 1, h, True)


def per_device(front_init, green_hist, field_hist):
    n = lax.axis_size("col")
    if lax.axis_size("row") != 2 * n or green_hist.shape[3] != 2 * front_init.shape[3]:
        raise ValueError("unexpected mesh")
    count, orbits, parts, lanes = front_init.shape
    rows = count * orbits
    chunks = max(1, min(MOST_CHUNKS, rows // (8 * n), 2 * rows // lanes))
    unit = rows // (chunks * n)

    def flat(history):
        steps, depth = history.shape[:2]
        return history.reshape(steps * depth, parts, 2, lanes).transpose(0, 2, 1, 3).reshape(-1, lanes)

    def vmem(*shape):
        return pltpu.VMEM(shape, jnp.float32)

    depth = green_hist.shape[0] * green_hist.shape[1]
    lead = (ITERS, chunks)
    sems = lambda *shape: pltpu.SemaphoreType.DMA(shape)
    result = pl.pallas_call(
        functools.partial(kernel, n, chunks, orbits),
        out_shape=jax.ShapeDtypeStruct((rows * parts, lanes), jnp.float32),
        in_specs=[pl.BlockSpec(memory_space=pltpu.HBM)] * 3,
        out_specs=pl.BlockSpec(memory_space=pltpu.VMEM),
        scratch_shapes=[
            vmem(rows * parts, lanes),
            vmem(4 * depth, lanes),
            vmem(4 * depth, lanes),
            sems(3),
            pltpu.VMEM((2, 4 * depth, 2 * lanes), jnp.bfloat16),
            pltpu.VMEM((2, 4 * depth, 2 * lanes), jnp.bfloat16),
            vmem(*lead, 2, rows // chunks, lanes),
            vmem(*lead, 2, rows // chunks, lanes),
            vmem(chunks, 2, rows // chunks, lanes),
            vmem(*lead, n, 2, unit, lanes),
            vmem(*lead, n, 2, unit, lanes),
            vmem(*lead, 2, unit, lanes),
            vmem(*lead, n, 2, unit, lanes),
            sems(*lead), sems(*lead),
            sems(*lead), sems(*lead),
            sems(*lead), sems(*lead),
        ],
        compiler_params=pltpu.CompilerParams(
            collective_id=0, has_side_effects=True, vmem_limit_bytes=VMEM_LIMIT
        ),
    )(front_init.reshape(rows * parts, lanes), flat(green_hist), flat(field_hist))
    return result.reshape(front_init.shape)


def solution(mesh):
    in_specs = (
        P(None, None, None, "row"),
        P("row", None, None, "col"),
        P("row", None, None, "col"),
    )
    out_specs = P(None, None, None, "row")
    return jax.shard_map(
        per_device, mesh=mesh, in_specs=in_specs, out_specs=out_specs, check_vma=False
    )
```

```python
import functools

import jax
import jax.numpy as jnp
from jax import lax
from jax.experimental import pallas as pl
from jax.experimental.pallas import tpu as pltpu
from jax.sharding import PartitionSpec as P

ITERS = 2
STEP_WEIGHT = 0.5
MOST_CHUNKS = 4
VMEM_LIMIT = 54784 * 1024
MESH = pl.DeviceIdType.MESH


def split(value):
    high = value.astype(jnp.bfloat16)
    low = (value - high.astype(jnp.float32)).astype(jnp.bfloat16)
    return high, low


def swap_orbits(real_part, imag_part, orbits):
    rows, lanes = real_part.shape
    blocks = lanes // orbits
    turned = jnp.concatenate([real_part, imag_part], axis=0).T
    pieces = [turned[at * orbits:(at + 1) * orbits] for at in range(blocks)]
    block_of_lane = lax.broadcasted_iota(jnp.int32, (orbits, lanes), 1) // orbits
    step = 1
    while step < blocks:
        low_side = (block_of_lane // step) % 2 == 0
        for at in range(blocks):
            if at & step:
                continue
            first, second = pieces[at], pieces[at + step]
            pieces[at] = jnp.where(low_side, first, pltpu.roll(second, step * orbits, 1))
            pieces[at + step] = jnp.where(low_side, pltpu.roll(first, lanes - step * orbits, 1), second)
        step *= 2
    whole = jnp.concatenate(pieces, axis=0)
    return whole[:rows], whole[rows:]


def cubic_sigma(real_part, imag_part, orbits):
    other_re, other_im = swap_orbits(real_part, imag_part, orbits)
    square_re = real_part * real_part - imag_part * imag_part
    square_im = 2.0 * real_part * imag_part
    return square_re * other_re + square_im * other_im, square_im * other_re - square_re * other_im


def expected(chunks, it, at, h):
    if at == 3:
        return 8.3 * (it + 1) + 5.2 / chunks * h
    start = 8.3 * it + (5.2 if it else 2.8) / chunks * h
    return start + ((0.0, 1.25, 3.5) if it else (0.0, 1.3, 3.3))[at]


def kernel(
    n, chunks, orbits,
    front_hbm, green_hbm, field_hbm, out_ref,
    front_ref, green_ref, field_ref, load_sem, b_high, b_low, pair_out, pair_in, own, rs_out, rs_in, total, done,
    pair_ss, pair_rs, rs_ss, rs_rs, done_ss, done_rs,
):
    row, plane = lax.axis_index("row"), lax.axis_index("col")
    chip, core = row // 2, row % 2
    rows, lanes = front_ref.shape[0] // 2, front_ref.shape[1]
    chunk_rows = rows // chunks
    unit = chunk_rows // n
    group = lanes // 2

    def at_chip(other):
        return (other * 2 + core, plane)

    sibling = (chip * 2 + 1 - core, plane)
    chips = [lax.rem(chip + d, n) for d in range(n)]
    planes = [lax.rem(plane + d, n) for d in range(n)]

    loads = [
        pltpu.make_async_copy(src, dst, load_sem.at[at])
        for at, (src, dst) in enumerate(((green_hbm, green_ref), (field_hbm, field_ref), (front_hbm, front_ref)))
    ]
    for load in loads:
        load.start()

    barrier = pltpu.get_barrier_semaphore()
    for source in [sibling] + [at_chip(chips[d]) for d in range(1, n)]:
        pl.semaphore_signal(barrier, inc=1, device_id=source, device_id_type=MESH)

    @pl.when(chip != plane)
    def _():
        for d in range(n):
            pl.semaphore_signal(barrier, inc=1, device_id=(chips[d] * 2 + core, chip), device_id_type=MESH)

    for load in loads:
        load.wait()
    depth = green_ref.shape[0] // 4

    def prepare(side):
        at = 0
        for history in (field_ref, green_ref):
            parts = []
            for part in range(2):
                halves = [history[pl.ds(2 * half + part, depth, stride=4), :] for half in range(2)]
                parts.append(jnp.where(core == side, halves[1], halves[0]))
            real_high, real_low = split(parts[0])
            imag_high, imag_low = split(parts[1])
            for store, re, im in ((b_high, real_high, imag_high), (b_low, real_low, imag_low)):
                store[side, at:at + depth, :lanes] = re
                store[side, at:at + depth, lanes:] = im
                store[side, at + depth:at + 2 * depth, :lanes] = -im
                store[side, at + depth:at + 2 * depth, lanes:] = re
            at += 2 * depth

    def remote(src, dst, send_sem, recv_sem, device):
        return pltpu.make_async_remote_copy(
            src_ref=src, dst_ref=dst, send_sem=send_sem, recv_sem=recv_sem, device_id=device, device_id_type=MESH
        )

    def pair_copy(it, h):
        return remote(pair_out.at[it, h], pair_in.at[it, h], pair_ss.at[it, h], pair_rs.at[it, h], sibling)

    def rs_copy(it, h, d):
        return remote(rs_out.at[it, h, d], rs_in.at[it, h, d], rs_ss.at[it, h], rs_rs.at[it, h], at_chip(chips[d]))

    def rs_all(it, h):
        most = pl.ds(1, n - 1)
        return remote(rs_out.at[it, h, most], rs_in.at[it, h, most], rs_ss.at[it, h], rs_rs.at[it, h], at_chip(chips[1]))

    def done_copy(it, h, d):
        to = (plane * 2 + core, planes[d])
        return remote(total.at[it, h], done.at[it, h, chip], done_ss.at[it, h], done_rs.at[it, h], to)

    def done_all(it, h, count):
        pieces = done.at[it, h, pl.ds(0, count)]
        return remote(pieces, pieces, done_ss.at[it, h], done_rs.at[it, h], sibling)

    def wait_done(it, h, send):
        @pl.when(chip != plane)
        def _():
            copy = done_all(it, h, n)
            copy.wait_send() if send else copy.wait_recv()

        @pl.when(chip == plane)
        def _():
            copy = done_all(it, h, n - 1)
            copy.wait_send() if send else copy.wait_recv()

    def front(h, part):
        return front_ref[pl.ds(2 * h * chunk_rows + part, chunk_rows, stride=2), :]

    def arrived(it, h, part):
        return jnp.concatenate([done[it, h, p, part] for p in range(n)], axis=0)

    def current(it, h):
        if it == 0:
            return front(h, 0), front(h, 1)
        return tuple(front(h, part) + STEP_WEIGHT * arrived(it - 1, h, part) for part in range(2))

    def multiply(it, h):
        real_part, imag_part = current(it, h)
        sigmas = [
            cubic_sigma(real_part[at:at + group], imag_part[at:at + group], orbits)
            for at in range(0, chunk_rows, group)
        ]
        sigma_re = jnp.concatenate([s[0] for s in sigmas], axis=0)
        sigma_im = jnp.concatenate([s[1] for s in sigmas], axis=0)
        high, low = split(jnp.concatenate([real_part, imag_part, sigma_re, sigma_im], axis=1))
        both = jnp.concatenate([high, low], axis=0)
        for side, store in enumerate((pair_out.at[it], own)):
            if it == 0 and h == 0:
                prepare(side)
            upper = jnp.dot(both, b_high[side], preferred_element_type=jnp.float32)
            image = upper[:chunk_rows] + upper[chunk_rows:]
            image = image + jnp.dot(high, b_low[side], preferred_element_type=jnp.float32)
            store[h, 0] = image[:, :lanes]
            store[h, 1] = image[:, lanes:]
            if store is not own:
                if it == 0 and h == 0:
                    pl.semaphore_wait(barrier, 2 * n - 1)
                pair_copy(it, h).start()

    def add_pair(it, h):
        pair_copy(it, h).wait_recv()
        for d in list(range(1, n)) + [0]:
            to = chips[d]
            place = pl.ds(pl.multiple_of(to * unit, unit), unit)
            for part in range(2):
                rs_out[it, h, d, part] = own[h, part, place, :] + pair_in[it, h, part, place, :]
            if d:
                rs_copy(it, h, d).start()

    def add_chips(it, h):
        rs_all(it, h).wait_recv()
        value = rs_out[it, h, 0]
        for d in range(1, n):
            value = value + rs_in[it, h, d]
        total[it, h] = value

        for d in sorted(range(1, n), key=lambda d: abs(2 * d - n)):
            done_copy(it, h, d).start()

        @pl.when(chip != plane)
        def _():
            done_copy(it, h, 0).start()

        @pl.when(chip == plane)
        def _():
            done[it, h, chip] = value

    def drain():
        for it in range(ITERS):
            for h in range(chunks):
                pair_copy(it, h).wait_send()
                rs_all(it, h).wait_send()
                if it < ITERS - 1:
                    wait_done(it, h, True)

    def finish(it, h):
        if it == ITERS - 1 and h == 0:
            drain()
        wait_done(it, h, False)
        if it < ITERS - 1:
            multiply(it + 1, h)
        if it == ITERS - 1:
            for part in range(2):
                place = pl.ds(2 * h * chunk_rows + part, chunk_rows, stride=2)
                out_ref[place, :] = front(h, part) + STEP_WEIGHT * arrived(it, h, part)

    stages = (multiply, add_pair, add_chips, finish)
    tasks = [
        (it, at, h)
        for it in range(ITERS) for at in range(len(stages)) for h in range(chunks)
        if it == 0 or at > 0
    ]
    tasks.sort(key=lambda task: expected(chunks, *task))
    for it, at, h in tasks:
        stages[at](it, h)

    for h in range(chunks):
        wait_done(ITERS - 1, h, True)


def per_device(front_init, green_hist, field_hist):
    n = lax.axis_size("col")
    if lax.axis_size("row") != 2 * n or green_hist.shape[3] != 2 * front_init.shape[3]:
        raise ValueError("unexpected mesh")
    count, orbits, parts, lanes = front_init.shape
    rows = count * orbits
    chunks = max(1, min(MOST_CHUNKS, rows // (8 * n), 2 * rows // lanes))
    unit = rows // (chunks * n)

    def flat(history):
        steps, depth = history.shape[:2]
        return history.reshape(steps * depth, parts, 2, lanes).transpose(0, 2, 1, 3).reshape(-1, lanes)

    def vmem(*shape):
        return pltpu.VMEM(shape, jnp.float32)

    depth = green_hist.shape[0] * green_hist.shape[1]
    lead = (ITERS, chunks)
    sems = lambda *shape: pltpu.SemaphoreType.DMA(shape)
    result = pl.pallas_call(
        functools.partial(kernel, n, chunks, orbits),
        out_shape=jax.ShapeDtypeStruct((rows * parts, lanes), jnp.float32),
        in_specs=[pl.BlockSpec(memory_space=pltpu.HBM)] * 3,
        out_specs=pl.BlockSpec(memory_space=pltpu.VMEM),
        scratch_shapes=[
            vmem(rows * parts, lanes),
            vmem(4 * depth, lanes),
            vmem(4 * depth, lanes),
            sems(3),
            pltpu.VMEM((2, 4 * depth, 2 * lanes), jnp.bfloat16),
            pltpu.VMEM((2, 4 * depth, 2 * lanes), jnp.bfloat16),
            vmem(*lead, 2, rows // chunks, lanes),
            vmem(*lead, 2, rows // chunks, lanes),
            vmem(chunks, 2, rows // chunks, lanes),
            vmem(*lead, n, 2, unit, lanes),
            vmem(*lead, n, 2, unit, lanes),
            vmem(*lead, 2, unit, lanes),
            vmem(*lead, n, 2, unit, lanes),
            sems(*lead), sems(*lead),
            sems(*lead), sems(*lead),
            sems(*lead), sems(*lead),
        ],
        compiler_params=pltpu.CompilerParams(
            collective_id=0, has_side_effects=True, vmem_limit_bytes=VMEM_LIMIT
        ),
    )(front_init.reshape(rows * parts, lanes), flat(green_hist), flat(field_hist))
    return result.reshape(front_init.shape)


def solution(mesh):
    in_specs = (
        P(None, None, None, "row"),
        P("row", None, None, "col"),
        P("row", None, None, "col"),
    )
    out_specs = P(None, None, None, "row")
    return jax.shard_map(
        per_device, mesh=mesh, in_specs=in_specs, out_specs=out_specs, check_vma=False
    )
```
